32 devices in a mesh: band: 4 (over y, x), plane: 8 (over z, core).
Axes of the slice: x: 2, y: 2, z: 4, core: 2. Of those that a mesh axis runs over, the one named last changes fastest.
Arguments:
- orbitals: float32 [32, 96, 9216], P('band', 'plane'), may hold values from -6 to 6
Outputs:
- exchange_action: float32 [32, 96, 9216], P('band', 'plane')
The draws below stay inside these ranges and needn't reach their ends.
All inputs are finite; a program needn't handle non-finite values.
Results may differ from the reference program's by a relative error of at most 0.0001.
Values sent between devices are 32-bit elements; how exact they have to be, the bound alone decides.
No kernel may reach another device: no remote copies, remote signals or barrier semaphores. Data moves between devices by JAX's collectives and lax.ppermute only.
A program may use at most 192 MiB of HBM per device.

```python
import math
import jax
import jax.numpy as jnp
from jax import lax

NG = 96
LB = 8
PAIR = 2
ROUNDS = 4
NBANDS = 32


def block_scale(own_key, shape, cuts, low, largest):
    loudness, own = 1.0, jax.random.fold_in(own_key, 6)
    for dim, shards_of in cuts:
        heights = jnp.exp(jax.random.uniform(jax.random.fold_in(own, dim), (shards_of,), jnp.float32, low / len(cuts), largest / len(cuts)))
        loudness = loudness * jnp.repeat(heights, shape[dim] // shards_of).reshape([-1 if axis == dim else 1 for axis in range(len(shape))])
    return loudness


def noise(rng, dims, spread, limit, shards=(), held_as=jnp.bfloat16):
    factor_of = block_scale(rng, dims, shards, -0.22, 0.18) if shards else 1.0
    array = jax.random.normal(rng, dims, jnp.float32) * spread * factor_of
    return jnp.minimum(jnp.maximum(array, -limit), limit).astype(held_as)


def setup_inputs(seed: int = 0) -> dict:
    keys = jax.random.split(jax.random.key(seed), 2)
    return {
        "orbitals": noise(keys[0], (NBANDS, NG, NG * NG), 1.0, 6.0, ((0, 4), (1, 8)), jnp.float32),
    }


OMEGA = 0.106
CELL = 41.05
ALPHA = 0.25


def frequencies(count):
    index = jnp.arange(count)
    return jnp.where(index <= count // 2, index, index - count).astype(jnp.float32)


def screened(count):
    freq = frequencies(count)
    square = freq * freq
    scale = (2.0 * math.pi / CELL) ** 2
    g_two = scale * (square[:, None, None] + square[None, :, None] + square[None, None, :])
    positive = g_two > 0
    safe = jnp.where(positive, g_two, 1.0)
    value = 4.0 * math.pi / safe * (-jnp.expm1(-safe / (4.0 * OMEGA * OMEGA)))
    return jnp.where(positive, value, math.pi / (OMEGA * OMEGA))


def reference(orbitals):
    nbands = orbitals.shape[0]
    fields = orbitals.reshape(nbands, NG, NG, NG)
    kernel = screened(NG)

    def solve(density):
        return jnp.real(jnp.fft.ifftn(kernel * jnp.fft.fftn(density)))

    total = jnp.zeros_like(fields)
    for turn in range(ROUNDS):
        for member in range(PAIR):
            partner_index = turn * LB + member
            partner = fields[partner_index]

            def single_pair(single):
                potential = solve(single * partner).astype(fields.dtype)
                return partner * potential, single * potential

            near_terms, far_terms = lax.map(single_pair, fields)
            total = total + near_terms
            total = total.at[partner_index].add(jnp.sum(far_terms, axis=0))
    return (-ALPHA * total).reshape(nbands, NG, NG * NG)
```

```python
import functools
import math

import jax
import jax.numpy as jnp
import numpy as np
from jax import lax
from jax.experimental import pallas as pl
from jax.experimental.pallas import tpu as pltpu
from jax.sharding import Mesh, PartitionSpec as P

PAIR = 2
ROUNDS = 4
OMEGA = 0.106
CELL = 41.05
ALPHA = 0.25
LANES = 128
F32 = jnp.float32
BF16 = jnp.bfloat16


def hartley_table(count):
    index = np.arange(count)
    angle = (index[:, None] * index[None, :] % count).astype(np.float64) * (2.0 * math.pi / count)
    return (np.cos(angle) + np.sin(angle)).astype(np.float32)


def halves(value):
    high = value.astype(BF16)
    return high, (value - high.astype(F32)).astype(BF16)


def np_halves(value):
    high = value.astype(BF16)
    return high, (value - high.astype(np.float32)).astype(BF16)


def row_order(count):
    return np.arange(count).reshape(count // 4, 4).T.reshape(-1)


def lane_table(count):
    table = np.zeros((LANES, LANES), np.float32)
    table[:count, :count] = hartley_table(count)
    high, low = np_halves(table)
    top = np.concatenate([high, low], axis=1)
    return np.concatenate([top, np.concatenate([high, np.zeros_like(low)], axis=1)], axis=0)


def row_table(table):
    high, low = np_halves(table)
    top = np.concatenate([high, high], axis=1)
    return np.concatenate([top, np.concatenate([low, np.zeros_like(low)], axis=1)], axis=0)


def frequencies(count):
    index = jnp.arange(count, dtype=jnp.int32)
    return jnp.where(index <= count // 2, index, index - count).astype(F32)


def screened_kernel(count):
    freq = frequencies(count)
    square = freq * freq
    scale = (2.0 * math.pi / CELL) ** 2
    wide = jnp.pad(square, (0, LANES - count))
    g_two = scale * (
        square.reshape(count // 2, 1, 2, 1) + square[None, :, None, None] + wide[None, None, None, :]
    )
    positive = g_two > 0
    safe = jnp.where(positive, g_two, 1.0)
    value = 4.0 * math.pi / safe * -jnp.expm1(-safe / (4.0 * OMEGA * OMEGA))
    value = jnp.where(positive, value, math.pi / (OMEGA * OMEGA))
    return (value / float(count**3)).reshape(count // 2, count, 2 * LANES)


def to_rows(parts):
    first, second, third = parts
    lane = lax.broadcasted_iota(jnp.int32, first.shape, 1)
    row1 = jnp.where(lane < 32, pltpu.roll(first, 32, 1), pltpu.roll(second, 32, 1))
    row2 = jnp.where(lane < 64, pltpu.roll(second, 64, 1), pltpu.roll(third, 64, 1))
    row3 = pltpu.roll(third, 96, 1)
    return jnp.concatenate([first, row1, row2, row3], axis=0)


def from_rows(plane):
    step = plane.shape[0] // 4
    row0, row1, row2, row3 = (plane[k * step : (k + 1) * step] for k in range(4))
    lane = lax.broadcasted_iota(jnp.int32, row0.shape, 1)
    first = jnp.where(lane < 96, row0, pltpu.roll(row1, 96, 1))
    second = jnp.where(lane < 64, pltpu.roll(row1, 96, 1), pltpu.roll(row2, 64, 1))
    third = jnp.where(lane < 32, pltpu.roll(row2, 64, 1), pltpu.roll(row3, 32, 1))
    return first, second, third


def dot(a, b):
    return jnp.dot(a, b, preferred_element_type=F32)


def along_lanes(value, table):
    out = dot(jnp.concatenate(halves(value), axis=1), table)
    return out[:, :LANES] + out[:, LANES:]


def along_rows(table, value):
    out = dot(table, jnp.concatenate(halves(value), axis=0))
    half = out.shape[0] // 2
    return out[:half] + out[half:]


def pair_kernel(
    count, partner, orbital, acc_in, lanes, rows_in, rows_mid, rows_out, coulomb, acc, owner, field
):
    third = count // 4

    def density(x):
        parts = []
        for r in range(3):
            place = pl.ds(r * third, third)
            parts.append(orbital[0, x, place, :] * partner[0, x, place, :])
        return to_rows(parts)

    def forward(step, carry):
        x = 2 * step
        both = jnp.concatenate([density(x), density(x + 1)], axis=0)
        both = along_lanes(both, lanes[...])
        both = jnp.concatenate([both[:count], both[count:]], axis=1)
        both = along_rows(rows_in[...], both)
        start = pl.multiple_of(x * count, 2 * count)
        field[pl.ds(start, count), :] = both[:, :LANES]
        field[pl.ds(start + count, count), :] = both[:, LANES:]
        return carry

    lax.fori_loop(0, count // 2, forward, 0)

    def middle(step, carry):
        v = 2 * step
        both = jnp.concatenate(
            [field[pl.ds(v, count, stride=count), :], field[pl.ds(v + 1, count, stride=count), :]], axis=1
        )
        both = along_rows(rows_mid[...], both) * coulomb[step]
        both = along_rows(rows_mid[...], both)
        field[pl.ds(v, count, stride=count), :] = both[:, :LANES]
        field[pl.ds(v + 1, count, stride=count), :] = both[:, LANES:]
        return carry

    lax.fori_loop(0, count // 2, middle, 0)

    first = pl.program_id(0) == 0

    def backward(step, carry):
        x = 2 * step
        start = pl.multiple_of(x * count, 2 * count)
        both = jnp.concatenate([field[pl.ds(start, count), :], field[pl.ds(start + count, count), :]], axis=1)
        both = along_rows(rows_out[...], both)
        both = along_lanes(jnp.concatenate([both[:, :LANES], both[:, LANES:]], axis=0), lanes[...])
        for k in range(2):
            for r, part in enumerate(from_rows(both[k * count : (k + 1) * count])):
                place = pl.ds(r * third, third)
                acc[0, x + k, place, :] = acc_in[0, x + k, place, :] + partner[0, x + k, place, :] * part
                term = orbital[0, x + k, place, :] * part
                owner[0, x + k, place, :] = jnp.where(first, 0.0, owner[0, x + k, place, :]) + term
        return carry

    lax.fori_loop(0, count // 2, backward, 0)


def pair_solve(partner, orbitals, acc, tables):
    lanes, rows_in, rows_mid, rows_out, coulomb = tables
    number, count, rows, _ = orbitals.shape
    block = (1, count, rows, LANES)
    one = pl.BlockSpec(block, lambda i: (0, 0, 0, 0), pipeline_mode=pl.Buffered(1))
    each = pl.BlockSpec(block, lambda i: (i, 0, 0, 0))
    whole = lambda a: pl.BlockSpec(a.shape, lambda i: (0,) * a.ndim, pipeline_mode=pl.Buffered(1))
    return pl.pallas_call(
        functools.partial(pair_kernel, count),
        grid=(number,),
        in_specs=[one, each, each] + [whole(t) for t in tables],
        out_specs=[each, pl.BlockSpec(block, lambda i: (0, 0, 0, 0))],
        out_shape=[jax.ShapeDtypeStruct(orbitals.shape, F32), jax.ShapeDtypeStruct(partner.shape, F32)],
        scratch_shapes=[pltpu.VMEM((count * count, LANES), F32)],
        input_output_aliases={2: 0},
        cost_estimate=pl.CostEstimate(
            flops=number * 36 * count**3 * LANES, bytes_accessed=16 * number * count * rows * LANES, transcendentals=0
        ),
        compiler_params=pltpu.CompilerParams(vmem_limit_bytes=60 * 1024 * 1024),
    )(partner, orbitals, acc, lanes, rows_in, rows_mid, rows_out, coulomb)


def make_tables(count):
    table = hartley_table(count)
    order = row_order(count)
    return (
        jnp.asarray(lane_table(count)),
        jnp.asarray(row_table(table[:, order])),
        jnp.asarray(row_table(table)),
        jnp.asarray(row_table(table[order, :])),
        screened_kernel(count),
    )


def pack(fields):
    number, planes, flat = fields.shape
    return fields.reshape(number, planes, flat // 384, 3, LANES).swapaxes(2, 3).reshape(number, planes, flat // LANES, LANES)


def unpack(fields):
    number, planes, rows, _ = fields.shape
    return fields.reshape(number, planes, 3, rows // 3, LANES).swapaxes(2, 3).reshape(number, planes, rows * LANES)


def local(orbitals):
    packed = pack(orbitals)
    n_local, planes, rows, _ = packed.shape
    zs = lax.axis_size("z")
    count = planes * zs * 2
    tables = make_tables(count)
    tail = (rows, LANES)
    core = lax.axis_index("core")

    mine = lax.all_to_all(packed[0:PAIR], "core", split_axis=0, concat_axis=1, tiled=True)
    partners = lax.all_gather(mine, ("band", "z"), axis=0, tiled=False)
    bands = lax.axis_size("band")
    partners = partners.reshape((bands, count) + tail)

    split = lax.all_to_all(packed, "z", split_axis=0, concat_axis=1, tiled=True)
    own = n_local // zs
    whole = lax.all_gather(split.reshape((own, zs, planes) + tail), "core", axis=2, tiled=False)
    whole = whole.reshape((own, count) + tail)

    acc = jnp.zeros_like(whole)
    terms = []
    for turn in range(ROUNDS):
        acc, term = pair_solve(partners[turn : turn + 1], whole, acc, tables)
        terms.append(term)
    terms += [jnp.zeros_like(terms[0])] * (bands - ROUNDS)
    owner = jnp.concatenate(terms, axis=0).reshape((bands * zs, 2 * planes) + tail)
    owner = lax.psum_scatter(owner, ("band", "z"), scatter_dimension=0, tiled=True)
    owner = lax.all_to_all(owner.reshape((1, 2 * planes) + tail), "core", split_axis=1, concat_axis=0, tiled=True)

    acc = acc.reshape((own, zs, 2, planes) + tail)
    acc = lax.psum_scatter(acc, "core", scatter_dimension=2, tiled=False)
    acc = acc.reshape((own, zs * planes) + tail)
    acc = lax.all_to_all(acc, "z", split_axis=1, concat_axis=0, tiled=True)
    acc = acc.at[0:PAIR].add(owner)
    return -ALPHA * unpack(acc)


def solution(mesh):
    bands, planes = mesh.devices.shape
    inner = Mesh(mesh.devices.reshape(bands, planes // 2, 2), ("band", "z", "core"))
    placed = P("band", ("z", "core"), None)
    return jax.shard_map(local, mesh=inner, in_specs=(placed,), out_specs=placed, check_vma=False)
```

```python
import functools
import math

import jax
import jax.numpy as jnp
import numpy as np
from jax import lax
from jax.experimental import pallas as pl
from jax.experimental.pallas import tpu as pltpu
from jax.sharding import Mesh, PartitionSpec as P

PAIR = 2
ROUNDS = 4
OMEGA = 0.106
CELL = 41.05
ALPHA = 0.25
LANES = 128
F32 = jnp.float32
BF16 = jnp.bfloat16
GROUP = 8


def hartley_table(count):
    index = np.arange(count)
    angle = (index[:, None] * index[None, :] % count).astype(np.float64) * (2.0 * math.pi / count)
    return (np.cos(angle) + np.sin(angle)).astype(np.float32)


def halves(value):
    high = value.astype(BF16)
    return high, (value - high.astype(F32)).astype(BF16)


def np_halves(value):
    high = value.astype(BF16)
    return high, (value - high.astype(np.float32)).astype(BF16)


def row_order(count):
    return np.arange(count).reshape(count // 4, 4).T.reshape(-1)


def lane_table(count):
    table = np.zeros((LANES, LANES), np.float32)
    table[:count, :count] = hartley_table(count)
    high, low = np_halves(table)
    top = np.concatenate([high, low], axis=1)
    return np.concatenate([top, np.concatenate([high, np.zeros_like(low)], axis=1)], axis=0)


def row_table(table):
    high, low = np_halves(table)
    top = np.concatenate([high, high], axis=1)
    return np.concatenate([top, np.concatenate([low, np.zeros_like(low)], axis=1)], axis=0)


def frequencies(count):
    index = jnp.arange(count, dtype=jnp.int32)
    return jnp.where(index <= count // 2, index, index - count).astype(F32)


def screened_kernel(count):
    freq = frequencies(count)
    square = freq * freq
    scale = (2.0 * math.pi / CELL) ** 2
    wide = jnp.pad(square, (0, LANES - count))
    g_two = scale * (
        square.reshape(count // 2, 1, 2, 1) + square[None, :, None, None] + wide[None, None, None, :]
    )
    positive = g_two > 0
    safe = jnp.where(positive, g_two, 1.0)
    value = 4.0 * math.pi / safe * -jnp.expm1(-safe / (4.0 * OMEGA * OMEGA))
    value = jnp.where(positive, value, math.pi / (OMEGA * OMEGA))
    return (value / float(count**3)).reshape(count // 2, count, 2 * LANES)


def to_rows(parts):
    first, second, third = parts
    lane = lax.broadcasted_iota(jnp.int32, first.shape, 1)
    row1 = jnp.where(lane < 32, pltpu.roll(first, 32, 1), pltpu.roll(second, 32, 1))
    row2 = jnp.where(lane < 64, pltpu.roll(second, 64, 1), pltpu.roll(third, 64, 1))
    row3 = pltpu.roll(third, 96, 1)
    return jnp.concatenate([first, row1, row2, row3], axis=0)


def from_rows(plane):
    step = plane.shape[0] // 4
    row0, row1, row2, row3 = (plane[k * step : (k + 1) * step] for k in range(4))
    lane = lax.broadcasted_iota(jnp.int32, row0.shape, 1)
    first = jnp.where(lane < 96, row0, pltpu.roll(row1, 96, 1))
    second = jnp.where(lane < 64, pltpu.roll(row1, 96, 1), pltpu.roll(row2, 64, 1))
    third = jnp.where(lane < 32, pltpu.roll(row2, 64, 1), pltpu.roll(row3, 32, 1))
    return first, second, third


def dot(a, b):
    return jnp.dot(a, b, preferred_element_type=F32)


def along_lanes(value, table):
    out = dot(jnp.concatenate(halves(value), axis=1), table)
    return out[:, :LANES] + out[:, LANES:]


def along_rows(table, value):
    out = dot(table, jnp.concatenate(halves(value), axis=0))
    half = out.shape[0] // 2
    return out[:half] + out[half:]


def pair_kernel(
    count, fresh, partner, orbital, *refs
):
    acc_in = None if fresh else refs[0]
    lanes, rows_in, rows_mid, rows_out, coulomb, acc, owner, field = refs[-8:]
    third = count // 4

    def density(x):
        parts = []
        for r in range(3):
            place = pl.ds(r * third, third)
            parts.append(orbital[0, x, place, :] * partner[0, x, place, :])
        return to_rows(parts)

    def forward(step, carry):
        base = 2 * GROUP * step
        pairs = [
            jnp.concatenate([density(base + 2 * g), density(base + 2 * g + 1)], axis=0) for g in range(GROUP)
        ]
        pairs = [along_lanes(both, lanes[...]) for both in pairs]
        pairs = [jnp.concatenate([both[:count], both[count:]], axis=1) for both in pairs]
        pairs = [along_rows(rows_in[...], both) for both in pairs]
        start = pl.multiple_of(base * count, 2 * count)
        for g, both in enumerate(pairs):
            field[pl.ds(start + 2 * g * count, count), :] = both[:, :LANES]
            field[pl.ds(start + (2 * g + 1) * count, count), :] = both[:, LANES:]
        return carry

    lax.fori_loop(0, count // 2 // GROUP, forward, 0)

    def middle(step, carry):
        base = 2 * GROUP * step
        pairs = [
            jnp.concatenate(
                [field[pl.ds(base + 2 * g + k, count, stride=count), :] for k in range(2)], axis=1
            )
            for g in range(GROUP)
        ]
        pairs = [along_rows(rows_mid[...], both) for both in pairs]
        pairs = [both * coulomb[GROUP * step + g] for g, both in enumerate(pairs)]
        pairs = [along_rows(rows_mid[...], both) for both in pairs]
        for g, both in enumerate(pairs):
            for k in range(2):
                field[pl.ds(base + 2 * g + k, count, stride=count), :] = both[:, k * LANES : (k + 1) * LANES]
        return carry

    lax.fori_loop(0, count // 2 // GROUP, middle, 0)

    first = pl.program_id(0) == 0

    def backward(step, carry):
        base = 2 * GROUP * step
        start = pl.multiple_of(base * count, 2 * count)
        pairs = [
            jnp.concatenate([field[pl.ds(start + (2 * g + k) * count, count), :] for k in range(2)], axis=1)
            for g in range(GROUP)
        ]
        pairs = [along_rows(rows_out[...], both) for both in pairs]
        pairs = [jnp.concatenate([both[:, :LANES], both[:, LANES:]], axis=0) for both in pairs]
        pairs = [along_lanes(both, lanes[...]) for both in pairs]
        for g, both in enumerate(pairs):
            for k in range(2):
                x = base + 2 * g + k
                for r, part in enumerate(from_rows(both[k * count : (k + 1) * count])):
                    place = pl.ds(r * third, third)
                    near = partner[0, x, place, :] * part
                    acc[0, x, place, :] = near if fresh else acc_in[0, x, place, :] + near
                    term = orbital[0, x, place, :] * part
                    owner[0, x, place, :] = jnp.where(first, 0.0, owner[0, x, place, :]) + term
        return carry

    lax.fori_loop(0, count // 2 // GROUP, backward, 0)


def pair_solve(partner, orbitals, acc, tables):
    number, count, rows, _ = orbitals.shape
    block = (1, count, rows, LANES)
    one = pl.BlockSpec(block, lambda i: (0, 0, 0, 0), pipeline_mode=pl.Buffered(1))
    each = pl.BlockSpec(block, lambda i: (i, 0, 0, 0))
    whole = lambda a: pl.BlockSpec(a.shape, lambda i: (0,) * a.ndim, pipeline_mode=pl.Buffered(1))
    fresh = acc is None
    start = () if fresh else (acc,)
    return pl.pallas_call(
        functools.partial(pair_kernel, count, fresh),
        grid=(number,),
        in_specs=[one, each] + [each] * len(start) + [whole(t) for t in tables],
        out_specs=[each, pl.BlockSpec(block, lambda i: (0, 0, 0, 0))],
        out_shape=[jax.ShapeDtypeStruct(orbitals.shape, F32), jax.ShapeDtypeStruct(partner.shape, F32)],
        scratch_shapes=[pltpu.VMEM((count * count, LANES), F32)],
        input_output_aliases={} if fresh else {2: 0},
        cost_estimate=pl.CostEstimate(
            flops=number * 36 * count**3 * LANES, bytes_accessed=16 * number * count * rows * LANES, transcendentals=0
        ),
        compiler_params=pltpu.CompilerParams(vmem_limit_bytes=60 * 1024 * 1024),
    )(partner, orbitals, *start, *tables)


def make_tables(count):
    table = hartley_table(count)
    order = row_order(count)
    return (
        jnp.asarray(lane_table(count)),
        jnp.asarray(row_table(table[:, order])),
        jnp.asarray(row_table(table)),
        jnp.asarray(row_table(table[order, :])),
        screened_kernel(count),
    )


def piece_row(tile, rows):
    return tile % 3 * (rows // 3) + tile // 3


def pack_kernel(planes, rows, flat, packed):
    for tile in range(rows):
        row = piece_row(tile, rows)
        packed[0, pl.ds(row, planes, stride=rows), :] = flat[0, :, tile * LANES : (tile + 1) * LANES]


def pack(fields):
    number, planes, flat = fields.shape
    rows = flat // LANES
    packed = pl.pallas_call(
        functools.partial(pack_kernel, planes, rows),
        grid=(number,),
        in_specs=[pl.BlockSpec((1, planes, flat), lambda i: (i, 0, 0))],
        out_specs=pl.BlockSpec((1, planes * rows, LANES), lambda i: (i, 0, 0)),
        out_shape=jax.ShapeDtypeStruct((number, planes * rows, LANES), F32),
    )(fields)
    return packed.reshape(number, planes, rows, LANES)


def unpack_kernel(planes, rows, packed, extra, flat):
    more = jnp.where(pl.program_id(0) < PAIR, 1.0, 0.0)
    for tile in range(rows):
        place = pl.ds(piece_row(tile, rows), planes, stride=rows)
        value = packed[0, place, :] + more * extra[0, place, :]
        flat[0, :, tile * LANES : (tile + 1) * LANES] = -ALPHA * value


def unpack(fields, extra):
    number, planes, rows, _ = fields.shape
    block = (1, planes * rows, LANES)
    return pl.pallas_call(
        functools.partial(unpack_kernel, planes, rows),
        grid=(number,),
        in_specs=[
            pl.BlockSpec(block, lambda i: (i, 0, 0)),
            pl.BlockSpec(block, lambda i: (jnp.minimum(i, PAIR - 1), 0, 0)),
        ],
        out_specs=pl.BlockSpec((1, planes, rows * LANES), lambda i: (i, 0, 0)),
        out_shape=jax.ShapeDtypeStruct((number, planes, rows * LANES), F32),
    )(fields.reshape(number, planes * rows, LANES), extra.reshape(PAIR, planes * rows, LANES))


def swap(value, axis, flip):
    size = lax.axis_size(axis)
    return lax.ppermute(value, axis, [(i, i ^ flip) for i in range(size)])


def shift(value, step, low, high):
    return lax.ppermute(value, "z", [(z, z + step) for z in range(low, high + 1)])


def gather_line(slab):
    length = lax.axis_size("z")
    down, up = [slab], [slab]
    for step in range(1, length):
        down.append(shift(down[-1], 1, step - 1, length - 2))
        up.append(shift(up[-1], -1, 1, length - step))
    every = jnp.concatenate(down[:0:-1] + up, axis=0)
    size = slab.shape[0]
    start = (length - 1 - lax.axis_index("z")) * size
    return lax.dynamic_slice_in_dim(every, start, length * size, axis=0)


def scatter_line(field):
    length = lax.axis_size("z")
    size = field.shape[0] // length
    place = lax.axis_index("z")

    def block(offset):
        start = jnp.clip(place + offset, 0, length - 1) * size
        return lax.dynamic_slice_in_dim(field, start, size, axis=0)

    down = up = 0.0
    for step in range(length - 1, 0, -1):
        down = shift(block(step) + down, 1, 0, length - 1 - step)
        up = shift(block(-step) + up, -1, step, length - 1)
    return block(0) + down + up


def whole_orbitals(packed):
    n_local, planes, rows, _ = packed.shape
    zs, core = lax.axis_size("z"), lax.axis_index("core")
    mine = lax.all_to_all(packed, "z", split_axis=0, concat_axis=1, tiled=True)
    mine = mine.reshape(n_local // zs, zs, 1, planes, rows, LANES)
    other = swap(mine, "core", 1)
    whole = jnp.where(
        core == 0, jnp.concatenate([mine, other], axis=2), jnp.concatenate([other, mine], axis=2)
    )
    return whole.reshape(n_local // zs, zs * 2 * planes, rows, LANES)


def spread_sums(sums, planes):
    own, count, rows, _ = sums.shape
    zs, core = lax.axis_size("z"), lax.axis_index("core")
    sums = sums.reshape(own, zs, 2, planes, rows, LANES)
    keep = lax.dynamic_index_in_dim(sums, core, 2, keepdims=False)
    give = lax.dynamic_index_in_dim(sums, 1 - core, 2, keepdims=False)
    total = (keep + swap(give, "core", 1)).reshape(own, zs * planes, rows, LANES)
    return lax.all_to_all(total, "z", split_axis=1, concat_axis=0, tiled=True)


def local(orbitals):
    n_local, planes, flat = orbitals.shape
    zs, bands = lax.axis_size("z"), lax.axis_size("band")
    count = planes * zs * 2
    tables = make_tables(count)
    packed = pack(orbitals)
    tail = packed.shape[2:]
    slab = lax.all_to_all(packed[0:PAIR], "core", split_axis=0, concat_axis=1, tiled=True)[0]
    if bands == ROUNDS:
        own = gather_line(slab)
        side, far = swap(own, "band", 1), swap(own, "band", 2)
        cross = jnp.concatenate(
            [swap(side[: count // 2], "band", 2), swap(far[count // 2 :], "band", 1)], axis=0
        )
        partners = [own, side, far, cross]
    else:
        every = lax.all_gather(slab, ("band", "z"), axis=0, tiled=True)
        partners = list(every.reshape((bands, count) + tail)[:ROUNDS])
    whole = whole_orbitals(packed)
    sums = None
    terms = []
    for partner in partners:
        sums, term = pair_solve(partner[None], whole, sums, tables)
        terms.append(term[0])
    if bands == ROUNDS:
        owner = terms[0] + swap(terms[1], "band", 1) + swap(terms[2], "band", 2) + swap(terms[3], "band", 3)
        owner = scatter_line(owner)
    else:
        owner = jnp.concatenate(terms + [jnp.zeros_like(terms[0])] * (bands - ROUNDS), axis=0)
        owner = lax.psum_scatter(owner, ("band", "z"), scatter_dimension=0, tiled=True)
    owner = lax.all_to_all(owner[None], "core", split_axis=1, concat_axis=0, tiled=True)
    return unpack(spread_sums(sums, planes), owner)


def solution(mesh):
    bands, planes = mesh.devices.shape
    inner = Mesh(mesh.devices.reshape(bands, planes // 2, 2), ("band", "z", "core"))
    placed = P("band", ("z", "core"), None)
    return jax.shard_map(local, mesh=inner, in_specs=(placed,), out_specs=placed, check_vma=False)
```

```python
import functools
import math

import jax
import jax.numpy as jnp
import numpy as np
from jax import lax
from jax.experimental import pallas as pl
from jax.experimental.pallas import tpu as pltpu
from jax.sharding import Mesh, PartitionSpec as P

PAIR = 2
ROUNDS = 4
OMEGA = 0.106
CELL = 41.05
ALPHA = 0.25
LANES = 128
F32 = jnp.float32
BF16 = jnp.bfloat16
MIDDLE = 12
PIECES = 5
COST_BYTES = 1 << 20


def hartley_table(count):
    index = np.arange(count)
    angle = (index[:, None] * index[None, :] % count).astype(np.float64) * (2.0 * math.pi / count)
    return (np.cos(angle) + np.sin(angle)).astype(np.float32)


def halves(value):
    high = value.astype(BF16)
    return high, (value - high.astype(F32)).astype(BF16)


def np_halves(value):
    high = value.astype(BF16)
    return high, (value - high.astype(np.float32)).astype(BF16)


def row_order(count):
    return np.arange(count).reshape(count // 4, 4).T.reshape(-1)


def lane_table(count):
    table = np.zeros((LANES, LANES), np.float32)
    table[:count, :count] = hartley_table(count)
    high, low = np_halves(table)
    top = np.concatenate([high, low], axis=1)
    return np.concatenate([top, np.concatenate([high, np.zeros_like(low)], axis=1)], axis=0)


def row_table(table):
    high, low = np_halves(table)
    top = np.concatenate([high, high], axis=1)
    return np.concatenate([top, np.concatenate([low, np.zeros_like(low)], axis=1)], axis=0)


def screened_kernel(count):
    shape = (count // 2, count, 2 * LANES)

    def squared(axis, place):
        index = place(lax.broadcasted_iota(jnp.int32, shape, axis))
        freq = jnp.where(index <= count // 2, index, index - count).astype(F32)
        return freq * freq

    second = 2 * lax.broadcasted_iota(jnp.int32, shape, 0)
    second = second + (lax.broadcasted_iota(jnp.int32, shape, 2) >= LANES).astype(jnp.int32)
    scale = (2.0 * math.pi / CELL) ** 2
    g_two = scale * (squared(0, lambda i: second) + squared(1, lambda i: i) + squared(2, lambda i: i % LANES))
    positive = g_two > 0
    safe = jnp.where(positive, g_two, 1.0)
    value = 4.0 * math.pi / safe * -jnp.expm1(-safe / (4.0 * OMEGA * OMEGA))
    value = jnp.where(positive, value, math.pi / (OMEGA * OMEGA))
    return value / float(count**3)


def to_rows(parts):
    first, second, third = parts
    lane = lax.broadcasted_iota(jnp.int32, first.shape, 1)
    row1 = jnp.where(lane < 32, pltpu.roll(first, 32, 1), pltpu.roll(second, 32, 1))
    row2 = jnp.where(lane < 64, pltpu.roll(second, 64, 1), pltpu.roll(third, 64, 1))
    row3 = pltpu.roll(third, 96, 1)
    return jnp.concatenate([first, row1, row2, row3], axis=0)


def from_rows(plane):
    step = plane.shape[0] // 4
    row0, row1, row2, row3 = (plane[k * step : (k + 1) * step] for k in range(4))
    lane = lax.broadcasted_iota(jnp.int32, row0.shape, 1)
    first = jnp.where(lane < 96, row0, pltpu.roll(row1, 96, 1))
    second = jnp.where(lane < 64, pltpu.roll(row1, 96, 1), pltpu.roll(row2, 64, 1))
    third = jnp.where(lane < 32, pltpu.roll(row2, 64, 1), pltpu.roll(row3, 32, 1))
    return first, second, third


def dot(a, b):
    return jnp.dot(a, b, preferred_element_type=F32)


def along_lanes(value, table):
    out = dot(jnp.concatenate(halves(value), axis=1), table)
    return out[:, :LANES] + out[:, LANES:]


def along_rows(table, value):
    out = dot(table, jnp.concatenate(halves(value), axis=0))
    half = out.shape[0] // 2
    return out[:half] + out[half:]


def pair_kernel(count, sizes, layout, *refs):
    split_in, sums_in, sums_split, terms_in, split_out = layout
    zs, planes = sizes
    slab = 2 * planes
    third = count // 4
    refs = list(refs)
    place = refs.pop(0)
    partner_hbm = [refs.pop(0) for _ in range(PIECES if split_in else 1)]
    mine_hbm, other_hbm = refs.pop(0), refs.pop(0)
    sums_hbm = refs.pop(0) if sums_in else None
    terms_hbm = refs.pop(0) if terms_in else None
    tables_hbm, coulomb_hbm = refs.pop(0), refs.pop(0)
    sums_out = [refs.pop(0) for _ in range(2 if sums_split else 1)]
    terms_out = [refs.pop(0) for _ in range(PIECES if split_out else 1)]
    partner, orbital, sums, terms, field, tables, coulomb, sem, sem_c = refs
    lanes = tables.at[: 2 * LANES]
    rows_in, rows_mid, rows_out = (
        tables.at[pl.ds(2 * LANES + 2 * count * k, 2 * count), : 2 * count] for k in range(3)
    )
    z, core = place[0], place[1]

    def part(ref, index, size=slab):
        return ref.at[pl.ds(pl.multiple_of(index * size, size), size)]

    def pieces(refs_):
        spots = [(z, None), (z - 1, z >= 1), (z + 1, z < zs - 1), (z ^ 2, None), (3 - z, (z == 0) | (z == 3))]
        return [(ref, spot, there) for ref, (spot, there) in zip(refs_, spots)]

    def start(source, target, semaphore, there=None):
        def go():
            pltpu.make_async_copy(source, target, semaphore).start()

        if there is None:
            go()
        else:
            pl.when(there)(go)

    def wait(like_source, like_target, semaphore):
        pltpu.make_async_copy(like_source, like_target, semaphore).wait()

    start(tables_hbm, tables, sem_c.at[1])
    if split_in:
        for ref, spot, there in pieces(partner_hbm):
            start(ref, part(partner, spot), sem.at[0, spot], there)
    else:
        for s in range(zs):
            start(part(partner_hbm[0], s), part(partner, s), sem.at[0, s])
    for s in range(zs):
        start(mine_hbm.at[s], part(orbital, 2 * s + core, planes), sem.at[1, s])
        start(other_hbm.at[s], part(orbital, 2 * s + 1 - core, planes), sem.at[2, s])
    start(coulomb_hbm, coulomb, sem_c.at[0])
    for s in range(zs):
        if sums_in:
            start(part(sums_hbm, s), part(sums, s), sem.at[3, s])
        if terms_in:
            start(part(terms_hbm, s), part(terms, s), sem.at[4, s])

    def density(x):
        parts = []
        for r in range(3):
            rows = pl.ds(r * third, third)
            parts.append(orbital[x, rows, :] * partner[x, rows, :])
        return to_rows(parts)

    group = planes

    def forward(step, carry):
        wait(part(partner, step), part(partner, step), sem.at[0, step])
        wait(part(orbital, 2 * step, planes), part(orbital, 2 * step, planes), sem.at[1, step])
        wait(part(orbital, 2 * step, planes), part(orbital, 2 * step, planes), sem.at[2, step])
        base = 2 * group * step
        pairs = [jnp.concatenate([density(base + 2 * g), density(base + 2 * g + 1)], axis=0) for g in range(group)]
        pairs = [along_lanes(both, lanes[...]) for both in pairs]
        pairs = [jnp.concatenate([both[:count], both[count:]], axis=1) for both in pairs]
        pairs = [along_rows(rows_in[...], both) for both in pairs]
        begin = pl.multiple_of(base * count, 2 * count)
        for g, both in enumerate(pairs):
            field[pl.ds(begin + 2 * g * count, count), :] = both[:, :LANES]
            field[pl.ds(begin + (2 * g + 1) * count, count), :] = both[:, LANES:]
        return carry

    wait(tables_hbm, tables, sem_c.at[1])
    lax.fori_loop(0, zs, forward, 0)
    wait(coulomb_hbm, coulomb, sem_c.at[0])

    def middle(step, carry):
        base = 2 * MIDDLE * step
        pairs = [
            jnp.concatenate(
                [field[pl.ds(base + 2 * g + k, count, stride=count), :] for k in range(2)], axis=1
            )
            for g in range(MIDDLE)
        ]
        pairs = [along_rows(rows_mid[...], both) for both in pairs]
        pairs = [both * coulomb[MIDDLE * step + g] for g, both in enumerate(pairs)]
        pairs = [along_rows(rows_mid[...], both) for both in pairs]
        for g, both in enumerate(pairs):
            for k in range(2):
                field[pl.ds(base + 2 * g + k, count, stride=count), :] = both[:, k * LANES : (k + 1) * LANES]
        return carry

    lax.fori_loop(0, count // 2 // MIDDLE, middle, 0)

    def backward(step, carry):
        if sums_in:
            wait(part(sums_hbm, step), part(sums, step), sem.at[3, step])
        if terms_in:
            wait(part(terms_hbm, step), part(terms, step), sem.at[4, step])
        base = 2 * group * step
        begin = pl.multiple_of(base * count, 2 * count)
        pairs = [
            jnp.concatenate([field[pl.ds(begin + (2 * g + k) * count, count), :] for k in range(2)], axis=1)
            for g in range(group)
        ]
        pairs = [along_rows(rows_out[...], both) for both in pairs]
        pairs = [jnp.concatenate([both[:, :LANES], both[:, LANES:]], axis=0) for both in pairs]
        pairs = [along_lanes(both, lanes[...]) for both in pairs]
        for g, both in enumerate(pairs):
            for k in range(2):
                x = base + 2 * g + k
                for r, value in enumerate(from_rows(both[k * count : (k + 1) * count])):
                    rows = pl.ds(r * third, third)
                    near = partner[x, rows, :] * value
                    sums[x, rows, :] = sums[x, rows, :] + near if sums_in else near
                    far = orbital[x, rows, :] * value
                    terms[x, rows, :] = terms[x, rows, :] + far if terms_in else far
        if sums_split:
            start(part(sums, 2 * step + core, planes), sums_out[0].at[step], sem.at[5, step])
            start(part(sums, 2 * step + 1 - core, planes), sums_out[1].at[step], sem.at[6, step])
        else:
            start(part(sums, step), part(sums_out[0], step), sem.at[5, step])
        if split_out:
            for ref, spot, there in pieces(terms_out):
                start(part(terms, step), ref, sem.at[7, step], (spot == step) if there is None else (spot == step) & there)
        else:
            start(part(terms, step), part(terms_out[0], step), sem.at[7, step])
        return carry

    lax.fori_loop(0, zs, backward, 0)
    for s in range(zs):
        if sums_split:
            for k in range(2):
                wait(part(sums, s, planes), sums_out[k].at[s], sem.at[5 + k, s])
        else:
            wait(part(sums, s), part(sums_out[0], s), sem.at[5, s])
        target = terms_out[0] if split_out else part(terms_out[0], s)
        wait(part(terms, s), target, sem.at[7, s])


def pair_solve(place, partner, mine, other, sums, terms, tables, last_partner, last_orbital):
    zs, planes, rows, _ = mine.shape
    count = zs * 2 * planes
    split_in = len(partner) > 1
    layout = (split_in, sums is not None, last_partner, terms is not None, last_orbital and split_in)
    field = jax.ShapeDtypeStruct((count, rows, LANES), F32)
    kinds = [jax.ShapeDtypeStruct(mine.shape, F32)] * 2 if last_partner else [field]
    pieces = [jax.ShapeDtypeStruct(p.shape, F32) for p in partner] if layout[4] else [field]
    more = [a for a in (sums, terms) if a is not None]
    anywhere = pl.BlockSpec(memory_space=pltpu.HBM)
    block = (count, rows, LANES)
    out = pl.pallas_call(
        functools.partial(pair_kernel, count, (zs, planes), layout),
        in_specs=[pl.BlockSpec(memory_space=pltpu.SMEM)]
        + [anywhere] * (len(partner) + 4 + len(more)),
        out_specs=[anywhere] * (len(kinds) + len(pieces)),
        out_shape=kinds + pieces,
        scratch_shapes=[pltpu.VMEM(block, F32)] * 4
        + [
            pltpu.VMEM((count * count, LANES), F32),
            pltpu.VMEM(tables[0].shape, BF16),
            pltpu.VMEM(tables[1].shape, F32),
            pltpu.SemaphoreType.DMA((8, zs)),
            pltpu.SemaphoreType.DMA((2,)),
        ],
        cost_estimate=pl.CostEstimate(
            flops=12 * count**4, bytes_accessed=COST_BYTES, transcendentals=0
        ),
        compiler_params=pltpu.CompilerParams(vmem_limit_bytes=48 * 1024 * 1024),
    )(place, *partner, mine, other, *more, *tables)
    sums = out[:2] if last_partner else out[0]
    terms = out[len(kinds) :] if layout[4] else out[-1]
    return sums, terms


def make_tables(count):
    table = hartley_table(count)
    order = row_order(count)
    rows = [row_table(t) for t in (table[:, order], table, table[order, :])]
    rows = [np.pad(t, ((0, 0), (0, 2 * LANES - t.shape[1]))) for t in rows]
    return jnp.asarray(np.concatenate([lane_table(count)] + rows, axis=0)), screened_kernel(count)


def piece_row(tile, rows):
    return tile % 3 * (rows // 3) + tile // 3


def pack_kernel(sets, planes, rows, flat, *packed):
    size = flat.shape[1] // sets
    plane = pl.program_id(0)
    for tile in range(rows):
        row = plane * rows + piece_row(tile, rows)
        for k in range(sets):
            value = flat[0, k * size : (k + 1) * size, tile * LANES : (tile + 1) * LANES]
            packed[k][pl.ds(row, size, stride=planes * rows), :] = value


def pack(fields, sets):
    planes, number, flat = fields.shape
    rows, size = flat // LANES, number // sets
    out = (size * planes * rows, LANES)
    packed = pl.pallas_call(
        functools.partial(pack_kernel, sets, planes, rows),
        grid=(planes,),
        in_specs=[pl.BlockSpec((1, number, flat), lambda i: (i, 0, 0))],
        out_specs=[pl.BlockSpec(out, lambda i: (0, 0))] * sets,
        out_shape=[jax.ShapeDtypeStruct(out, F32)] * sets,
        compiler_params=pltpu.CompilerParams(vmem_limit_bytes=32 * 1024 * 1024),
    )(fields)
    return [p.reshape(size, planes, rows, LANES) for p in packed]


def unpack_kernel(sets, planes, rows, *refs):
    packed, extra, flat = refs[:sets], refs[sets], refs[-1]
    size = flat.shape[1] // sets
    plane = pl.program_id(0)
    for tile in range(rows):
        row = plane * rows + piece_row(tile, rows)
        more = extra[pl.ds(row, PAIR, stride=planes * rows), :]
        for k in range(sets):
            value = packed[k][pl.ds(row, size, stride=planes * rows), :]
            if k == 0:
                value = jnp.concatenate([value[:PAIR] + more, value[PAIR:]], axis=0)
            flat[0, k * size : (k + 1) * size, tile * LANES : (tile + 1) * LANES] = -ALPHA * value


def unpack(fields, extra):
    sets = len(fields)
    size, planes, rows, _ = fields[0].shape
    whole = lambda n: pl.BlockSpec((n * planes * rows, LANES), lambda i: (0, 0), pipeline_mode=pl.Buffered(1))
    return pl.pallas_call(
        functools.partial(unpack_kernel, sets, planes, rows),
        grid=(planes,),
        in_specs=[whole(size)] * sets + [whole(PAIR)],
        out_specs=pl.BlockSpec((1, sets * size, rows * LANES), lambda i: (i, 0, 0)),
        out_shape=jax.ShapeDtypeStruct((planes, sets * size, rows * LANES), F32),
        compiler_params=pltpu.CompilerParams(vmem_limit_bytes=32 * 1024 * 1024),
    )(*(f.reshape(size * planes * rows, LANES) for f in fields), extra.reshape(PAIR * planes * rows, LANES))


def swap(value, axis, flip):
    size = lax.axis_size(axis)
    return lax.ppermute(value, axis, [(i, i ^ flip) for i in range(size)])


def across(value, flip, chips):
    zs = lax.axis_size("z")
    pairs = [(b * zs + z, (b ^ flip) * zs + z) for b in range(lax.axis_size("band")) for z in chips]
    return lax.ppermute(value, ("band", "z"), pairs)


def along(value, pairs):
    return lax.ppermute(value, "z", pairs)


RIGHT = [(0, 1), (1, 2), (2, 3)]
LEFT = [(1, 0), (2, 1), (3, 2)]
THERE = ((0, 1, 2, 3), (1, 2, 3), (0, 1, 2), (0, 1, 2, 3), (0, 3))
EVEN = (True, False, False, True, False)


def gather_line(slab):
    before, after = along(slab, RIGHT), along(slab, LEFT)
    two = along(before, RIGHT[1:]) + along(after, LEFT[:2])
    three = along(two, [(2, 3), (1, 0)])
    return [slab, before, after, two, three]


def scatter_line(terms):
    slab, before, after, two, three = terms
    two = two + along(three, [(0, 1), (3, 2)])
    after = after + along(two, RIGHT[:2])
    before = before + along(two, LEFT[1:])
    return slab + along(after, RIGHT) + along(before, LEFT)


def spread(own):
    side, far, cross = [], [], []

    def send(out, piece, flip, chips, earlier):
        if len(earlier) > 1:
            piece, earlier[-2] = lax.optimization_barrier((piece, earlier[-2]))
        out.append(across(piece, flip, chips))

    for piece, chips in zip(own, THERE):
        send(side, piece, 1, chips, side)
        send(far, piece, 2, chips, far)
    cross = [
        across(s, 2, chips) if even else across(f, 1, chips) for s, f, chips, even in zip(side, far, THERE, EVEN)
    ]
    return [own, side, far, cross]


def collect(own, side, far, cross):
    out = [None] * PIECES
    for k in (4, 3, 2, 1, 0):
        handed = across(cross[k], 2 if EVEN[k] else 1, THERE[k])
        s, f = (side[k] + handed, far[k]) if EVEN[k] else (side[k], far[k] + handed)
        out[k] = own[k] + across(s, 1, THERE[k]) + across(f, 2, THERE[k])
    return out


def local(orbitals):
    n_local, planes, flat = orbitals.shape
    zs, bands, core = lax.axis_size("z"), lax.axis_size("band"), lax.axis_index("core")
    count = planes * zs * 2
    place = jnp.stack([lax.axis_index("z"), core]).astype(jnp.int32)
    tables = make_tables(count)
    sets = pack(orbitals.swapaxes(0, 1), n_local // zs)
    tail = sets[0].shape[2:]
    slab = lax.all_to_all(sets[0][:PAIR], "core", split_axis=0, concat_axis=1, tiled=True)[0]
    square = bands == ROUNDS == 4 and zs == 4
    if square:
        own = gather_line(slab)
        partners = spread(own)
        partners[:3] = lax.optimization_barrier(partners[:3])
        orders = [(0, 1, 2, 3), (3, 1, 2, 0)]
        ready = own[3]
    else:
        every = lax.all_gather(slab, ("band", "z"), axis=0, tiled=True).reshape((bands, count) + tail)
        partners = [[every[k]] for k in range(ROUNDS)]
        orders = [range(ROUNDS)] * len(sets)
        ready = slab
    mine = []
    for fields in sets:
        fields, ready = lax.optimization_barrier((fields, ready))
        ready = lax.all_to_all(fields, "z", split_axis=0, concat_axis=0, tiled=True)
        mine.append(ready)
    other = [swap(m, "core", 1) for m in mine]
    terms = [None] * ROUNDS
    spread_sums = []
    for k, order in zip(range(len(sets)), orders):
        sums = None
        for turn in order:
            sums, terms[turn] = pair_solve(
                place, partners[turn], mine[k], other[k], sums, terms[turn], tables, turn == order[-1], k == len(sets) - 1
            )
        keep, give = sums
        spread_sums.append(lax.all_to_all(keep + swap(give, "core", 1), "z", split_axis=0, concat_axis=0, tiled=True))
    if square:
        owner = scatter_line(collect(*terms))
    else:
        owner = jnp.concatenate([t[None] for t in terms] + [jnp.zeros((bands - ROUNDS, count) + tail, F32)], axis=0)
        owner = owner.reshape((bands * count,) + tail)
        owner = lax.psum_scatter(owner, ("band", "z"), scatter_dimension=0, tiled=True)
    owner = lax.all_to_all(owner[None], "core", split_axis=1, concat_axis=0, tiled=True)
    return unpack(spread_sums, owner).swapaxes(0, 1)


def solution(mesh):
    bands, planes = mesh.devices.shape
    inner = Mesh(mesh.devices.reshape(bands, planes // 2, 2), ("band", "z", "core"))
    placed = P("band", ("z", "core"), None)
    return jax.shard_map(local, mesh=inner, in_specs=(placed,), out_specs=placed, check_vma=False)
```

```python
import functools
import math

import jax
import jax.numpy as jnp
import numpy as np
from jax import lax
from jax.experimental import pallas as pl
from jax.experimental.pallas import tpu as pltpu
from jax.sharding import Mesh, PartitionSpec as P

PAIR = 2
ROUNDS = 4
OMEGA = 0.106
CELL = 41.05
ALPHA = 0.25
LANES = 128
F32 = jnp.float32
BF16 = jnp.bfloat16
MIDDLE = 12
PIECES = 4


def hartley_table(count):
    index = np.arange(count)
    angle = (index[:, None] * index[None, :] % count).astype(np.float64) * (2.0 * math.pi / count)
    return (np.cos(angle) + np.sin(angle)).astype(np.float32)


def halves(value):
    high = value.astype(BF16)
    return high, (value - high.astype(F32)).astype(BF16)


def np_halves(value):
    high = value.astype(BF16)
    return high, (value - high.astype(np.float32)).astype(BF16)


def row_order(count):
    return np.arange(count).reshape(count // 4, 4).T.reshape(-1)


def lane_table(count):
    table = np.zeros((LANES, LANES), np.float32)
    table[:count, :count] = hartley_table(count)
    high, low = np_halves(table)
    top = np.concatenate([high, low], axis=1)
    return np.concatenate([top, np.concatenate([high, np.zeros_like(low)], axis=1)], axis=0)


def row_table(table):
    high, low = np_halves(table)
    top = np.concatenate([high, high], axis=1)
    return np.concatenate([top, np.concatenate([low, np.zeros_like(low)], axis=1)], axis=0)


def screened_kernel(count):
    shape = (count // 2, count, 2 * LANES)

    def squared(axis, place):
        index = place(lax.broadcasted_iota(jnp.int32, shape, axis))
        freq = jnp.where(index <= count // 2, index, index - count).astype(F32)
        return freq * freq

    second = 2 * lax.broadcasted_iota(jnp.int32, shape, 0)
    second = second + (lax.broadcasted_iota(jnp.int32, shape, 2) >= LANES).astype(jnp.int32)
    scale = (2.0 * math.pi / CELL) ** 2
    g_two = scale * (squared(0, lambda i: second) + squared(1, lambda i: i) + squared(2, lambda i: i % LANES))
    positive = g_two > 0
    safe = jnp.where(positive, g_two, 1.0)
    value = 4.0 * math.pi / safe * -jnp.expm1(-safe / (4.0 * OMEGA * OMEGA))
    value = jnp.where(positive, value, math.pi / (OMEGA * OMEGA))
    return value / float(count**3)


def to_rows(parts):
    first, second, third = parts
    lane = lax.broadcasted_iota(jnp.int32, first.shape, 1)
    row1 = jnp.where(lane < 32, pltpu.roll(first, 32, 1), pltpu.roll(second, 32, 1))
    row2 = jnp.where(lane < 64, pltpu.roll(second, 64, 1), pltpu.roll(third, 64, 1))
    row3 = pltpu.roll(third, 96, 1)
    return jnp.concatenate([first, row1, row2, row3], axis=0)


def from_rows(plane):
    step = plane.shape[0] // 4
    row0, row1, row2, row3 = (plane[k * step : (k + 1) * step] for k in range(4))
    lane = lax.broadcasted_iota(jnp.int32, row0.shape, 1)
    first = jnp.where(lane < 96, row0, pltpu.roll(row1, 96, 1))
    second = jnp.where(lane < 64, pltpu.roll(row1, 96, 1), pltpu.roll(row2, 64, 1))
    third = jnp.where(lane < 32, pltpu.roll(row2, 64, 1), pltpu.roll(row3, 32, 1))
    return first, second, third


def dot(a, b):
    return jnp.dot(a, b, preferred_element_type=F32)


def along_lanes(value, table):
    out = dot(jnp.concatenate(halves(value), axis=1), table)
    return out[:, :LANES] + out[:, LANES:]


def along_rows(table, value):
    out = dot(table, jnp.concatenate(halves(value), axis=0))
    half = out.shape[0] // 2
    return out[:half] + out[half:]


def pair_kernel(count, sizes, layout, *refs):
    split_in, sums_in, sums_split, terms_in, split_out = layout
    zs, planes = sizes
    slab = 2 * planes
    third = count // 4
    refs = list(refs)
    place = refs.pop(0)
    partner_hbm = [refs.pop(0) for _ in range(PIECES if split_in else 1)]
    mine_hbm, other_hbm = refs.pop(0), refs.pop(0)
    sums_hbm = refs.pop(0) if sums_in else None
    terms_hbm = refs.pop(0) if terms_in else None
    tables_hbm, coulomb_hbm = refs.pop(0), refs.pop(0)
    sums_out = [refs.pop(0) for _ in range(2 if sums_split else 1)]
    terms_out = [refs.pop(0) for _ in range(PIECES if split_out else 1)]
    partner, orbital, sums, terms, field, tables, coulomb, sem, sem_c = refs
    lanes = tables.at[: 2 * LANES]
    rows_in, rows_mid, rows_out = (
        tables.at[pl.ds(2 * LANES + 2 * count * k, 2 * count), : 2 * count] for k in range(3)
    )
    z, core = place[0], place[1]

    def part(ref, index, size=slab):
        return ref.at[pl.ds(pl.multiple_of(index * size, size), size)]

    def pieces(refs_):
        near = jnp.where(z == 0, 1, z - 1)
        return list(zip(refs_, [z, near, z ^ 2, 6 - z - near - (z ^ 2)]))

    def start(source, target, semaphore, there=None):
        def go():
            pltpu.make_async_copy(source, target, semaphore).start()

        if there is None:
            go()
        else:
            pl.when(there)(go)

    def wait(like_source, like_target, semaphore):
        pltpu.make_async_copy(like_source, like_target, semaphore).wait()

    start(tables_hbm, tables, sem_c.at[1])
    if split_in:
        for ref, spot in pieces(partner_hbm):
            start(ref, part(partner, spot), sem.at[0, spot])
    else:
        for s in range(zs):
            start(part(partner_hbm[0], s), part(partner, s), sem.at[0, s])
    for s in range(zs):
        start(mine_hbm.at[s], part(orbital, 2 * s + core, planes), sem.at[1, s])
        start(other_hbm.at[s], part(orbital, 2 * s + 1 - core, planes), sem.at[2, s])
    start(coulomb_hbm, coulomb, sem_c.at[0])
    for s in range(zs):
        if sums_in:
            start(part(sums_hbm, s), part(sums, s), sem.at[3, s])
        if terms_in:
            start(part(terms_hbm, s), part(terms, s), sem.at[4, s])

    def density(x):
        parts = []
        for r in range(3):
            rows = pl.ds(r * third, third)
            parts.append(orbital[x, rows, :] * partner[x, rows, :])
        return to_rows(parts)

    group = planes

    def forward(step, carry):
        wait(part(partner, step), part(partner, step), sem.at[0, step])
        wait(part(orbital, 2 * step, planes), part(orbital, 2 * step, planes), sem.at[1, step])
        wait(part(orbital, 2 * step, planes), part(orbital, 2 * step, planes), sem.at[2, step])
        base = 2 * group * step
        pairs = [jnp.concatenate([density(base + 2 * g), density(base + 2 * g + 1)], axis=0) for g in range(group)]
        pairs = [along_lanes(both, lanes[...]) for both in pairs]
        pairs = [jnp.concatenate([both[:count], both[count:]], axis=1) for both in pairs]
        pairs = [along_rows(rows_in[...], both) for both in pairs]
        begin = pl.multiple_of(base * count, 2 * count)
        for g, both in enumerate(pairs):
            field[pl.ds(begin + 2 * g * count, count), :] = both[:, :LANES]
            field[pl.ds(begin + (2 * g + 1) * count, count), :] = both[:, LANES:]
        return carry

    wait(tables_hbm, tables, sem_c.at[1])
    lax.fori_loop(0, zs, forward, 0)
    wait(coulomb_hbm, coulomb, sem_c.at[0])

    def middle(step, carry):
        base = 2 * MIDDLE * step
        pairs = [
            jnp.concatenate(
                [field[pl.ds(base + 2 * g + k, count, stride=count), :] for k in range(2)], axis=1
            )
            for g in range(MIDDLE)
        ]
        pairs = [along_rows(rows_mid[...], both) for both in pairs]
        pairs = [both * coulomb[MIDDLE * step + g] for g, both in enumerate(pairs)]
        pairs = [along_rows(rows_mid[...], both) for both in pairs]
        for g, both in enumerate(pairs):
            for k in range(2):
                field[pl.ds(base + 2 * g + k, count, stride=count), :] = both[:, k * LANES : (k + 1) * LANES]
        return carry

    lax.fori_loop(0, count // 2 // MIDDLE, middle, 0)

    def backward(step, carry):
        if sums_in:
            wait(part(sums_hbm, step), part(sums, step), sem.at[3, step])
        if terms_in:
            wait(part(terms_hbm, step), part(terms, step), sem.at[4, step])
        base = 2 * group * step
        begin = pl.multiple_of(base * count, 2 * count)
        pairs = [
            jnp.concatenate([field[pl.ds(begin + (2 * g + k) * count, count), :] for k in range(2)], axis=1)
            for g in range(group)
        ]
        pairs = [along_rows(rows_out[...], both) for both in pairs]
        pairs = [jnp.concatenate([both[:, :LANES], both[:, LANES:]], axis=0) for both in pairs]
        pairs = [along_lanes(both, lanes[...]) for both in pairs]
        for g, both in enumerate(pairs):
            for k in range(2):
                x = base + 2 * g + k
                for r, value in enumerate(from_rows(both[k * count : (k + 1) * count])):
                    rows = pl.ds(r * third, third)
                    near = partner[x, rows, :] * value
                    sums[x, rows, :] = sums[x, rows, :] + near if sums_in else near
                    far = orbital[x, rows, :] * value
                    terms[x, rows, :] = terms[x, rows, :] + far if terms_in else far
        if sums_split:
            start(part(sums, 2 * step + core, planes), sums_out[0].at[step], sem.at[5, step])
            start(part(sums, 2 * step + 1 - core, planes), sums_out[1].at[step], sem.at[6, step])
        else:
            start(part(sums, step), part(sums_out[0], step), sem.at[5, step])
        if split_out:
            for ref, spot in pieces(terms_out):
                start(part(terms, step), ref, sem.at[7, step], spot == step)
        else:
            start(part(terms, step), part(terms_out[0], step), sem.at[7, step])
        return carry

    lax.fori_loop(0, zs, backward, 0)
    for s in range(zs):
        if sums_split:
            for k in range(2):
                wait(part(sums, s, planes), sums_out[k].at[s], sem.at[5 + k, s])
        else:
            wait(part(sums, s), part(sums_out[0], s), sem.at[5, s])
        target = terms_out[0] if split_out else part(terms_out[0], s)
        wait(part(terms, s), target, sem.at[7, s])


def pair_solve(place, partner, mine, other, sums, terms, tables, last_partner, last_orbital):
    zs, planes, rows, _ = mine.shape
    count = zs * 2 * planes
    split_in = len(partner) > 1
    layout = (split_in, sums is not None, last_partner, terms is not None, last_orbital and split_in)
    field = jax.ShapeDtypeStruct((count, rows, LANES), F32)
    kinds = [jax.ShapeDtypeStruct(mine.shape, F32)] * 2 if last_partner else [field]
    pieces = [jax.ShapeDtypeStruct(p.shape, F32) for p in partner] if layout[4] else [field]
    more = [a for a in (sums, terms) if a is not None]
    anywhere = pl.BlockSpec(memory_space=pl.ANY)
    block = (count, rows, LANES)
    out = pl.pallas_call(
        functools.partial(pair_kernel, count, (zs, planes), layout),
        in_specs=[pl.BlockSpec(memory_space=pltpu.SMEM)]
        + [anywhere] * (len(partner) + 4 + len(more)),
        out_specs=[anywhere] * (len(kinds) + len(pieces)),
        out_shape=kinds + pieces,
        scratch_shapes=[pltpu.VMEM(block, F32)] * 4
        + [
            pltpu.VMEM((count * count, LANES), F32),
            pltpu.VMEM(tables[0].shape, BF16),
            pltpu.VMEM(tables[1].shape, F32),
            pltpu.SemaphoreType.DMA((8, zs)),
            pltpu.SemaphoreType.DMA((2,)),
        ],
        cost_estimate=pl.CostEstimate(
            flops=12 * count**4, bytes_accessed=20 * count * rows * LANES, transcendentals=0
        ),
        compiler_params=pltpu.CompilerParams(vmem_limit_bytes=60 * 1024 * 1024),
    )(place, *partner, mine, other, *more, *tables)
    sums = out[:2] if last_partner else out[0]
    terms = out[len(kinds) :] if layout[4] else out[-1]
    return sums, terms


def make_tables(count):
    table = hartley_table(count)
    order = row_order(count)
    rows = [row_table(t) for t in (table[:, order], table, table[order, :])]
    rows = [np.pad(t, ((0, 0), (0, 2 * LANES - t.shape[1]))) for t in rows]
    return jnp.asarray(np.concatenate([lane_table(count)] + rows, axis=0)), screened_kernel(count)


def piece_row(tile, rows):
    return tile % 3 * (rows // 3) + tile // 3


def pack_kernel(sets, planes, rows, flat, *packed):
    size = flat.shape[1] // sets
    plane = pl.program_id(0)
    for tile in range(rows):
        row = plane * rows + piece_row(tile, rows)
        for k in range(sets):
            value = flat[0, k * size : (k + 1) * size, tile * LANES : (tile + 1) * LANES]
            packed[k][pl.ds(row, size, stride=planes * rows), :] = value


def pack(fields, sets):
    planes, number, flat = fields.shape
    rows, size = flat // LANES, number // sets
    out = (size * planes * rows, LANES)
    packed = pl.pallas_call(
        functools.partial(pack_kernel, sets, planes, rows),
        grid=(planes,),
        in_specs=[pl.BlockSpec((1, number, flat), lambda i: (i, 0, 0))],
        out_specs=[pl.BlockSpec(out, lambda i: (0, 0))] * sets,
        out_shape=[jax.ShapeDtypeStruct(out, F32)] * sets,
        compiler_params=pltpu.CompilerParams(vmem_limit_bytes=32 * 1024 * 1024),
    )(fields)
    return [p.reshape(size, planes, rows, LANES) for p in packed]


def unpack_kernel(sets, planes, rows, *refs):
    packed, extra, flat = refs[:sets], refs[sets], refs[-1]
    size = flat.shape[1] // sets
    plane = pl.program_id(0)
    for tile in range(rows):
        row = plane * rows + piece_row(tile, rows)
        more = extra[pl.ds(row, PAIR, stride=planes * rows), :]
        for k in range(sets):
            value = packed[k][pl.ds(row, size, stride=planes * rows), :]
            if k == 0:
                value = jnp.concatenate([value[:PAIR] + more, value[PAIR:]], axis=0)
            flat[0, k * size : (k + 1) * size, tile * LANES : (tile + 1) * LANES] = -ALPHA * value


def unpack(fields, extra):
    sets = len(fields)
    size, planes, rows, _ = fields[0].shape
    whole = lambda n: pl.BlockSpec((n * planes * rows, LANES), lambda i: (0, 0), pipeline_mode=pl.Buffered(1))
    return pl.pallas_call(
        functools.partial(unpack_kernel, sets, planes, rows),
        grid=(planes,),
        in_specs=[whole(size)] * sets + [whole(PAIR)],
        out_specs=pl.BlockSpec((1, sets * size, rows * LANES), lambda i: (i, 0, 0)),
        out_shape=jax.ShapeDtypeStruct((planes, sets * size, rows * LANES), F32),
        compiler_params=pltpu.CompilerParams(vmem_limit_bytes=32 * 1024 * 1024),
    )(*(f.reshape(size * planes * rows, LANES) for f in fields), extra.reshape(PAIR * planes * rows, LANES))


def swap(value, axis, flip):
    size = lax.axis_size(axis)
    return lax.ppermute(value, axis, [(i, i ^ flip) for i in range(size)])


def along(value, pairs):
    return lax.ppermute(value, "z", pairs)


def tie(values, done):
    return lax.optimization_barrier((values, done))[0]


RIGHT = [(0, 1), (1, 2), (2, 3)]
LEFT = [(1, 0), (2, 1), (3, 2)]


def spread(slab, first):
    z = lax.axis_index("z")
    side, far = [], []

    def both(piece):
        side.append(swap(piece, "band", 1))
        far.append(swap(piece, "band", 2))

    before, after = along(slab, RIGHT), along(slab, LEFT)
    both(slab)
    before, after = tie((before, after), (side[-1], far[-1], first))
    near = jnp.where(z == 0, after, before)
    two = along(before, RIGHT[1:]) + along(after, LEFT[:2])
    both(near)
    two = tie(two, (side[-1], far[-1]))
    both(two)
    rest = jnp.where((z == 0) | (z == 3), along(two, [(2, 3), (1, 0)]), after)
    rest = tie(rest, (side[-1], far[-1]))
    both(rest)
    cross = [swap(tie(piece, rest), "band", flip) for piece, flip in zip((side[0], far[1], side[2], far[3]), (2, 1, 2, 1))]
    return [[slab, near, two, rest], side, far, cross]


def hand_over(cross):
    first = [swap(cross[2], "band", 2), swap(cross[3], "band", 1)]
    later = [swap(tie(cross[0], first), "band", 2), swap(tie(cross[1], first), "band", 1)]
    return [later[0], later[1], first[0], first[1]]


def scatter_line(slab, near, two, rest, near_in, slab_in):
    z = lax.axis_index("z")
    two = tie(two + along(rest, [(0, 1), (3, 2)]), near_in)
    near = near + near_in[0] + near_in[1]
    after, before = along(two, RIGHT[:2]), along(two, LEFT[1:])
    after, before = tie((jnp.where(z == 0, near, rest + after), near + before), slab_in)
    return slab + slab_in[0] + slab_in[1] + along(after, RIGHT) + along(before, LEFT)


def local(orbitals):
    n_local, planes, flat = orbitals.shape
    zs, bands, core = lax.axis_size("z"), lax.axis_size("band"), lax.axis_index("core")
    count = planes * zs * 2
    place = jnp.stack([lax.axis_index("z"), core]).astype(jnp.int32)
    tables = make_tables(count)
    sets = pack(orbitals.swapaxes(0, 1), n_local // zs)
    tail = sets[0].shape[2:]
    keep = lax.dynamic_index_in_dim(sets[0], core, 0, keepdims=False)
    come = swap(lax.dynamic_index_in_dim(sets[0], 1 - core, 0, keepdims=False), "core", 1)
    slab = jnp.concatenate([jnp.where(core == 0, keep, come), jnp.where(core == 0, come, keep)], axis=0)
    square = bands == ROUNDS == 4 and zs == 4 and len(sets) == 2
    if square:
        return square_local(place, tables, sets, slab)
    every = lax.all_gather(slab, ("band", "z"), axis=0, tiled=True).reshape((bands, count) + tail)
    terms = [None] * ROUNDS
    sums_out = []
    for k, fields in enumerate(sets):
        mine = lax.all_to_all(fields, "z", split_axis=0, concat_axis=0, tiled=True)
        other = swap(mine, "core", 1)
        sums = None
        for turn in range(ROUNDS):
            sums, terms[turn] = pair_solve(
                place, [every[turn]], mine, other, sums, terms[turn], tables, turn == ROUNDS - 1, k == len(sets) - 1
            )
        sums_out.append(sums)
    owner = jnp.concatenate([t[None] for t in terms] + [jnp.zeros((bands - ROUNDS, count) + tail, F32)], axis=0)
    owner = owner.reshape((bands * count,) + tail)
    owner = lax.psum_scatter(owner, ("band", "z"), scatter_dimension=0, tiled=True)
    return finish([send_back(core_sum(*sums)) for sums in sums_out], owner)


def core_sum(keep, give):
    return keep + swap(give, "core", 1)


def send_back(total):
    return lax.all_to_all(total, "z", split_axis=0, concat_axis=0, tiled=True)


def finish(sums, owner):
    core, planes = lax.axis_index("core"), owner.shape[0] // 2
    keep = lax.dynamic_slice_in_dim(owner, core * planes, planes)
    come = swap(lax.dynamic_slice_in_dim(owner, (1 - core) * planes, planes), "core", 1)
    owner = jnp.stack([jnp.where(core == 0, keep, come), jnp.where(core == 0, come, keep)])
    return unpack(sums, owner).swapaxes(0, 1)


def square_local(place, tables, sets, slab):
    first = lax.all_to_all(sets[0], "z", split_axis=0, concat_axis=0, tiled=True)
    partners = spread(slab, first)
    mine, other = [first], [swap(first, "core", 1)]

    def pair(k, turn, sums, term=None, after=None, last=False):
        partner = partners[turn] if after is None else tie(partners[turn], after)
        return pair_solve(place, partner, mine[k], other[k], sums, term, tables, last, k == 1)

    terms = [None] * ROUNDS
    sums, terms[0] = pair(0, 0, None, after=partners[1][:3] + partners[2][:3])
    mine.append(lax.all_to_all(tie(sets[1], terms[0]), "z", split_axis=0, concat_axis=0, tiled=True))
    other.append(swap(mine[1], "core", 1))
    sums, terms[1] = pair(0, 1, sums)
    sums, terms[2] = pair(0, 2, sums)
    sums, terms[3] = pair(0, 3, sums, last=True)
    back = [send_back(core_sum(*sums))]
    sums, cross = pair(1, 3, None, terms[3])
    handed = hand_over(cross)
    sums, side = pair(1, 1, sums, terms[1])
    sums, far = pair(1, 2, sums, terms[2], after=handed[2:])
    side = [side[0] + handed[0], side[1], side[2] + handed[2], side[3]]
    far = [far[0], far[1] + handed[1], far[2], far[3] + handed[3]]
    sent = swap(side[3], "band", 1)
    sums, own = pair(1, 0, sums, terms[0], after=[sent] + handed[:2], last=True)
    total = core_sum(*sums)
    back.append(send_back(total))
    arrived = [(swap(side[k], "band", 1), swap(far[k], "band", 2)) for k in range(PIECES - 1)]
    rest = own[3] + sent + swap(far[3], "band", 2)
    two = tie(own[2] + arrived[2][0] + arrived[2][1], total)
    return finish(back, scatter_line(own[0], own[1], two, rest, arrived[1], arrived[0]))


def solution(mesh):
    bands, planes = mesh.devices.shape
    inner = Mesh(mesh.devices.reshape(bands, planes // 2, 2), ("band", "z", "core"))
    placed = P("band", ("z", "core"), None)
    return jax.shard_map(local, mesh=inner, in_specs=(placed,), out_specs=placed, check_vma=False)
```

```python
import functools
import math

import jax
import jax.numpy as jnp
import numpy as np
from jax import lax
from jax.experimental import pallas as pl
from jax.experimental.pallas import tpu as pltpu
from jax.sharding import Mesh, PartitionSpec as P

PAIR = 2
ROUNDS = 4
OMEGA = 0.106
CELL = 41.05
ALPHA = 0.25
LANES = 128
F32 = jnp.float32
BF16 = jnp.bfloat16
MIDDLE = 12
GAP = 8
PIECES = 4


def hartley_table(count):
    index = np.arange(count)
    angle = (index[:, None] * index[None, :] % count).astype(np.float64) * (2.0 * math.pi / count)
    return (np.cos(angle) + np.sin(angle)).astype(np.float32)


def halves(value):
    high = value.astype(BF16)
    return high, (value - high.astype(F32)).astype(BF16)


def np_halves(value):
    high = value.astype(BF16)
    return high, (value - high.astype(np.float32)).astype(BF16)


def row_order(count):
    return np.arange(count).reshape(count // 4, 4).T.reshape(-1)


def lane_table(count):
    table = np.zeros((LANES, LANES), np.float32)
    table[:count, :count] = hartley_table(count)
    high, low = np_halves(table)
    top = np.concatenate([high, low], axis=1)
    return np.concatenate([top, np.concatenate([high, np.zeros_like(low)], axis=1)], axis=0)


def row_table(table):
    high, low = np_halves(table)
    top = np.concatenate([high, high], axis=1)
    return np.concatenate([top, np.concatenate([low, np.zeros_like(low)], axis=1)], axis=0)


def screened_kernel(count):
    shape = (count // 2, count, 2 * LANES)

    def squared(axis, place):
        index = place(lax.broadcasted_iota(jnp.int32, shape, axis))
        freq = jnp.where(index <= count // 2, index, index - count).astype(F32)
        return freq * freq

    second = 2 * lax.broadcasted_iota(jnp.int32, shape, 0)
    second = second + (lax.broadcasted_iota(jnp.int32, shape, 2) >= LANES).astype(jnp.int32)
    scale = (2.0 * math.pi / CELL) ** 2
    g_two = scale * (squared(0, lambda i: second) + squared(1, lambda i: i) + squared(2, lambda i: i % LANES))
    positive = g_two > 0
    safe = jnp.where(positive, g_two, 1.0)
    value = 4.0 * math.pi / safe * -jnp.expm1(-safe / (4.0 * OMEGA * OMEGA))
    value = jnp.where(positive, value, math.pi / (OMEGA * OMEGA))
    return value / float(count**3)


def to_rows(parts):
    first, second, third = parts
    lane = lax.broadcasted_iota(jnp.int32, first.shape, 1)
    row1 = jnp.where(lane < 32, pltpu.roll(first, 32, 1), pltpu.roll(second, 32, 1))
    row2 = jnp.where(lane < 64, pltpu.roll(second, 64, 1), pltpu.roll(third, 64, 1))
    row3 = pltpu.roll(third, 96, 1)
    return jnp.concatenate([first, row1, row2, row3], axis=0)


def from_rows(plane):
    step = plane.shape[0] // 4
    row0, row1, row2, row3 = (plane[k * step : (k + 1) * step] for k in range(4))
    lane = lax.broadcasted_iota(jnp.int32, row0.shape, 1)
    first = jnp.where(lane < 96, row0, pltpu.roll(row1, 96, 1))
    second = jnp.where(lane < 64, pltpu.roll(row1, 96, 1), pltpu.roll(row2, 64, 1))
    third = jnp.where(lane < 32, pltpu.roll(row2, 64, 1), pltpu.roll(row3, 32, 1))
    return first, second, third


def dot(a, b):
    return jnp.dot(a, b, preferred_element_type=F32)


def along_lanes(value, table):
    out = dot(jnp.concatenate(halves(value), axis=1), table)
    return out[:, :LANES] + out[:, LANES:]


def along_rows(table, value):
    out = dot(table, jnp.concatenate(halves(value), axis=0))
    half = out.shape[0] // 2
    return out[:half] + out[half:]


def pair_kernel(count, sizes, layout, *refs):
    split_in, sums_in, sums_split, terms_in, split_out = layout
    zs, planes = sizes
    slab = 2 * planes
    third, pitch = count // 4, count + GAP
    refs = list(refs)
    place = refs.pop(0)
    partner_hbm = [refs.pop(0) for _ in range(PIECES if split_in else 1)]
    mine_hbm, other_hbm = refs.pop(0), refs.pop(0)
    sums_hbm = refs.pop(0) if sums_in else None
    terms_hbm = refs.pop(0) if terms_in else None
    tables_hbm, coulomb_hbm = refs.pop(0), refs.pop(0)
    sums_out = [refs.pop(0) for _ in range(2 if sums_split else 1)]
    terms_out = [refs.pop(0) for _ in range(PIECES if split_out else 1)]
    partner, orbital, sums, terms, field, tables, coulomb, sem, sem_c = refs
    lanes = tables.at[: 2 * LANES]
    rows_in, rows_mid, rows_out = (
        tables.at[pl.ds(2 * LANES + 2 * count * k, 2 * count), : 2 * count] for k in range(3)
    )
    z, core = place[0], place[1]

    def part(ref, index, size=slab):
        return ref.at[pl.ds(pl.multiple_of(index * size, size), size)]

    def pieces(refs_):
        near = jnp.where(z == 0, 1, z - 1)
        return list(zip(refs_, [z, near, z ^ 2, 6 - z - near - (z ^ 2)]))

    def start(source, target, semaphore, there=None):
        def go():
            pltpu.make_async_copy(source, target, semaphore).start()

        if there is None:
            go()
        else:
            pl.when(there)(go)

    def wait(like_source, like_target, semaphore):
        pltpu.make_async_copy(like_source, like_target, semaphore).wait()

    start(tables_hbm, tables, sem_c.at[1])

    def load(s):
        if split_in:
            for ref, spot in pieces(partner_hbm):
                start(ref, part(partner, s), sem.at[0, s], spot == s)
        else:
            start(part(partner_hbm[0], s), part(partner, s), sem.at[0, s])
        start(mine_hbm.at[s], part(orbital, 2 * s + core, planes), sem.at[1, s])
        start(other_hbm.at[s], part(orbital, 2 * s + 1 - core, planes), sem.at[2, s])

    load(0)
    load(1)

    def density(x):
        parts = []
        for r in range(3):
            rows = pl.ds(r * third, third)
            parts.append(orbital[x, rows, :] * partner[x, rows, :])
        return to_rows(parts)

    group = planes

    def forward(step, carry):
        wait(part(partner, step), part(partner, step), sem.at[0, step])
        wait(part(orbital, 2 * step, planes), part(orbital, 2 * step, planes), sem.at[1, step])
        wait(part(orbital, 2 * step, planes), part(orbital, 2 * step, planes), sem.at[2, step])
        pl.when(step + 2 < zs)(lambda: load(step + 2))
        pl.when(step == zs - 2)(lambda: start(coulomb_hbm, coulomb, sem_c.at[0]))
        base = 2 * group * step
        pairs = [jnp.concatenate([density(base + 2 * g), density(base + 2 * g + 1)], axis=0) for g in range(group)]
        pairs = [along_lanes(both, lanes[...]) for both in pairs]
        pairs = [jnp.concatenate([both[:count], both[count:]], axis=1) for both in pairs]
        pairs = [along_rows(rows_in[...], both) for both in pairs]
        begin = pl.multiple_of(base * pitch, 2 * pitch)
        for g, both in enumerate(pairs):
            field[pl.ds(begin + 2 * g * pitch, count), :] = both[:, :LANES]
            field[pl.ds(begin + (2 * g + 1) * pitch, count), :] = both[:, LANES:]
        return carry

    wait(tables_hbm, tables, sem_c.at[1])
    lax.fori_loop(0, zs, forward, 0)
    for s in range(zs):
        if sums_in:
            start(part(sums_hbm, s), part(sums, s), sem.at[3, s])
        if terms_in:
            start(part(terms_hbm, s), part(terms, s), sem.at[4, s])
    wait(coulomb_hbm, coulomb, sem_c.at[0])

    def middle(step, carry):
        base = 2 * MIDDLE * step
        pairs = [
            jnp.concatenate(
                [field[pl.ds(base + 2 * g + k, count, stride=pitch), :] for k in range(2)], axis=1
            )
            for g in range(MIDDLE)
        ]
        pairs = [along_rows(rows_mid[...], both) for both in pairs]
        pairs = [both * coulomb[MIDDLE * step + g] for g, both in enumerate(pairs)]
        pairs = [along_rows(rows_mid[...], both) for both in pairs]
        for g, both in enumerate(pairs):
            for k in range(2):
                field[pl.ds(base + 2 * g + k, count, stride=pitch), :] = both[:, k * LANES : (k + 1) * LANES]
        return carry

    lax.fori_loop(0, count // 2 // MIDDLE, middle, 0)

    def backward(step, carry):
        if sums_in:
            wait(part(sums_hbm, step), part(sums, step), sem.at[3, step])
        if terms_in:
            wait(part(terms_hbm, step), part(terms, step), sem.at[4, step])
        base = 2 * group * step
        begin = pl.multiple_of(base * pitch, 2 * pitch)
        pairs = [
            jnp.concatenate([field[pl.ds(begin + (2 * g + k) * pitch, count), :] for k in range(2)], axis=1)
            for g in range(group)
        ]
        pairs = [along_rows(rows_out[...], both) for both in pairs]
        pairs = [jnp.concatenate([both[:, :LANES], both[:, LANES:]], axis=0) for both in pairs]
        pairs = [along_lanes(both, lanes[...]) for both in pairs]
        for g, both in enumerate(pairs):
            for k in range(2):
                x = base + 2 * g + k
                for r, value in enumerate(from_rows(both[k * count : (k + 1) * count])):
                    rows = pl.ds(r * third, third)
                    near = partner[x, rows, :] * value
                    sums[x, rows, :] = sums[x, rows, :] + near if sums_in else near
                    far = orbital[x, rows, :] * value
                    terms[x, rows, :] = terms[x, rows, :] + far if terms_in else far
        if sums_split:
            start(part(sums, 2 * step + core, planes), sums_out[0].at[step], sem.at[5, step])
            start(part(sums, 2 * step + 1 - core, planes), sums_out[1].at[step], sem.at[6, step])
        else:
            start(part(sums, step), part(sums_out[0], step), sem.at[5, step])
        if split_out:
            for ref, spot in pieces(terms_out):
                start(part(terms, step), ref, sem.at[7, step], spot == step)
        else:
            start(part(terms, step), part(terms_out[0], step), sem.at[7, step])
        return carry

    lax.fori_loop(0, zs, backward, 0)
    for s in range(zs):
        if sums_split:
            for k in range(2):
                wait(part(sums, s, planes), sums_out[k].at[s], sem.at[5 + k, s])
        else:
            wait(part(sums, s), part(sums_out[0], s), sem.at[5, s])
        target = terms_out[0] if split_out else part(terms_out[0], s)
        wait(part(terms, s), target, sem.at[7, s])


def pair_solve(place, partner, mine, other, sums, terms, tables, last_partner, last_orbital):
    zs, planes, rows, _ = mine.shape
    count = zs * 2 * planes
    split_in = len(partner) > 1
    layout = (split_in, sums is not None, last_partner, terms is not None, last_orbital and split_in)
    field = jax.ShapeDtypeStruct((count, rows, LANES), F32)
    kinds = [jax.ShapeDtypeStruct(mine.shape, F32)] * 2 if last_partner else [field]
    pieces = [jax.ShapeDtypeStruct(p.shape, F32) for p in partner] if layout[4] else [field]
    more = [a for a in (sums, terms) if a is not None]
    anywhere = pl.BlockSpec(memory_space=pl.ANY)
    block = (count, rows, LANES)
    out = pl.pallas_call(
        functools.partial(pair_kernel, count, (zs, planes), layout),
        in_specs=[pl.BlockSpec(memory_space=pltpu.SMEM)]
        + [anywhere] * (len(partner) + 4 + len(more)),
        out_specs=[anywhere] * (len(kinds) + len(pieces)),
        out_shape=kinds + pieces,
        scratch_shapes=[pltpu.VMEM(block, F32)] * 4
        + [
            pltpu.VMEM((count * (count + GAP), LANES), F32),
            pltpu.VMEM(tables[0].shape, BF16),
            pltpu.VMEM(tables[1].shape, F32),
            pltpu.SemaphoreType.DMA((8, zs)),
            pltpu.SemaphoreType.DMA((2,)),
        ],
        cost_estimate=pl.CostEstimate(
            flops=12 * count**4, bytes_accessed=20 * count * rows * LANES, transcendentals=0
        ),
        compiler_params=pltpu.CompilerParams(vmem_limit_bytes=60 * 1024 * 1024),
    )(place, *partner, mine, other, *more, *tables)
    sums = out[:2] if last_partner else out[0]
    terms = out[len(kinds) :] if layout[4] else out[-1]
    return sums, terms


def make_tables(count):
    table = hartley_table(count)
    order = row_order(count)
    rows = [row_table(t) for t in (table[:, order], table, table[order, :])]
    rows = [np.pad(t, ((0, 0), (0, 2 * LANES - t.shape[1]))) for t in rows]
    return jnp.asarray(np.concatenate([lane_table(count)] + rows, axis=0)), screened_kernel(count)


def piece_row(tile, rows):
    return tile % 3 * (rows // 3) + tile // 3


def pack_kernel(sets, planes, rows, flat, *packed):
    size = flat.shape[1] // sets
    plane = pl.program_id(0)
    for tile in range(rows):
        row = plane * rows + piece_row(tile, rows)
        for k in range(sets):
            value = flat[0, k * size : (k + 1) * size, tile * LANES : (tile + 1) * LANES]
            packed[k][pl.ds(row, size, stride=planes * rows), :] = value


def pack(fields, sets):
    planes, number, flat = fields.shape
    rows, size = flat // LANES, number // sets
    out = (size * planes * rows, LANES)
    packed = pl.pallas_call(
        functools.partial(pack_kernel, sets, planes, rows),
        grid=(planes,),
        in_specs=[pl.BlockSpec((1, number, flat), lambda i: (i, 0, 0))],
        out_specs=[pl.BlockSpec(out, lambda i: (0, 0))] * sets,
        out_shape=[jax.ShapeDtypeStruct(out, F32)] * sets,
        compiler_params=pltpu.CompilerParams(vmem_limit_bytes=32 * 1024 * 1024),
    )(fields)
    return [p.reshape(size, planes, rows, LANES) for p in packed]


def unpack_kernel(sets, planes, rows, *refs):
    packed, extra, flat = refs[:sets], refs[sets], refs[-1]
    size = flat.shape[1] // sets
    plane = pl.program_id(0)
    for tile in range(rows):
        row = plane * rows + piece_row(tile, rows)
        more = extra[pl.ds(row, PAIR, stride=planes * rows), :]
        for k in range(sets):
            value = packed[k][pl.ds(row, size, stride=planes * rows), :]
            if k == 0:
                value = jnp.concatenate([value[:PAIR] + more, value[PAIR:]], axis=0)
            flat[0, k * size : (k + 1) * size, tile * LANES : (tile + 1) * LANES] = -ALPHA * value


def unpack(fields, extra):
    sets = len(fields)
    size, planes, rows, _ = fields[0].shape
    whole = lambda n: pl.BlockSpec((n * planes * rows, LANES), lambda i: (0, 0), pipeline_mode=pl.Buffered(1))
    return pl.pallas_call(
        functools.partial(unpack_kernel, sets, planes, rows),
        grid=(planes,),
        in_specs=[whole(size)] * sets + [whole(PAIR)],
        out_specs=pl.BlockSpec((1, sets * size, rows * LANES), lambda i: (i, 0, 0)),
        out_shape=jax.ShapeDtypeStruct((planes, sets * size, rows * LANES), F32),
        compiler_params=pltpu.CompilerParams(vmem_limit_bytes=32 * 1024 * 1024),
    )(*(f.reshape(size * planes * rows, LANES) for f in fields), extra.reshape(PAIR * planes * rows, LANES))


def swap(value, axis, flip):
    size = lax.axis_size(axis)
    return lax.ppermute(value, axis, [(i, i ^ flip) for i in range(size)])


def along(value, pairs):
    return lax.ppermute(value, "z", pairs)


def tie(values, done):
    return lax.optimization_barrier((values, done))[0]


RIGHT = [(0, 1), (1, 2), (2, 3)]
LEFT = [(1, 0), (2, 1), (3, 2)]


def spread(slab, first):
    z = lax.axis_index("z")
    side, far = [], []

    def both(piece):
        side.append(swap(piece, "band", 1))
        far.append(swap(piece, "band", 2))

    before, after = along(slab, RIGHT), along(slab, LEFT)
    both(slab)
    before, after = tie((before, after), (side[-1], far[-1], first))
    near = jnp.where(z == 0, after, before)
    two = along(before, RIGHT[1:]) + along(after, LEFT[:2])
    both(near)
    two = tie(two, (side[-1], far[-1]))
    both(two)
    rest = jnp.where((z == 0) | (z == 3), along(two, [(2, 3), (1, 0)]), after)
    rest = tie(rest, (side[-1], far[-1]))
    both(rest)
    cross = [swap(tie(piece, rest), "band", flip) for piece, flip in zip((side[0], far[1], side[2], far[3]), (2, 1, 2, 1))]
    return [[slab, near, two, rest], side, far, cross]


def hand_over(cross):
    first = [swap(cross[2], "band", 2), swap(cross[3], "band", 1)]
    later = [swap(tie(cross[0], first), "band", 2), swap(tie(cross[1], first), "band", 1)]
    return [later[0], later[1], first[0], first[1]]


def scatter_line(slab, near, two, rest, near_in, slab_in):
    z = lax.axis_index("z")
    two = tie(two + along(rest, [(0, 1), (3, 2)]), near_in)
    near = near + near_in[0] + near_in[1]
    after, before = along(two, RIGHT[:2]), along(two, LEFT[1:])
    after, before = tie((jnp.where(z == 0, near, rest + after), near + before), slab_in)
    return slab + slab_in[0] + slab_in[1] + along(after, RIGHT) + along(before, LEFT)


def local(orbitals):
    n_local, planes, flat = orbitals.shape
    zs, bands, core = lax.axis_size("z"), lax.axis_size("band"), lax.axis_index("core")
    count = planes * zs * 2
    place = jnp.stack([lax.axis_index("z"), core]).astype(jnp.int32)
    tables = make_tables(count)
    sets = pack(orbitals.swapaxes(0, 1), n_local // zs)
    tail = sets[0].shape[2:]
    keep = lax.dynamic_index_in_dim(sets[0], core, 0, keepdims=False)
    come = swap(lax.dynamic_index_in_dim(sets[0], 1 - core, 0, keepdims=False), "core", 1)
    slab = jnp.concatenate([jnp.where(core == 0, keep, come), jnp.where(core == 0, come, keep)], axis=0)
    square = bands == ROUNDS == 4 and zs == 4 and len(sets) == 2
    if square:
        return square_local(place, tables, sets, slab)
    every = lax.all_gather(slab, ("band", "z"), axis=0, tiled=True).reshape((bands, count) + tail)
    terms = [None] * ROUNDS
    sums_out = []
    for k, fields in enumerate(sets):
        mine = lax.all_to_all(fields, "z", split_axis=0, concat_axis=0, tiled=True)
        other = swap(mine, "core", 1)
        sums = None
        for turn in range(ROUNDS):
            sums, terms[turn] = pair_solve(
                place, [every[turn]], mine, other, sums, terms[turn], tables, turn == ROUNDS - 1, k == len(sets) - 1
            )
        sums_out.append(sums)
    owner = jnp.concatenate([t[None] for t in terms] + [jnp.zeros((bands - ROUNDS, count) + tail, F32)], axis=0)
    owner = owner.reshape((bands * count,) + tail)
    owner = lax.psum_scatter(owner, ("band", "z"), scatter_dimension=0, tiled=True)
    return finish([send_back(core_sum(*sums)) for sums in sums_out], owner)


def core_sum(keep, give):
    return keep + swap(give, "core", 1)


def send_back(total):
    return lax.all_to_all(total, "z", split_axis=0, concat_axis=0, tiled=True)


def finish(sums, owner):
    core, planes = lax.axis_index("core"), owner.shape[0] // 2
    keep = lax.dynamic_slice_in_dim(owner, core * planes, planes)
    come = swap(lax.dynamic_slice_in_dim(owner, (1 - core) * planes, planes), "core", 1)
    owner = jnp.stack([jnp.where(core == 0, keep, come), jnp.where(core == 0, come, keep)])
    return unpack(sums, owner).swapaxes(0, 1)


def square_local(place, tables, sets, slab):
    first = lax.all_to_all(sets[0], "z", split_axis=0, concat_axis=0, tiled=True)
    partners = spread(slab, first)
    mine, other = [first], [swap(first, "core", 1)]

    def pair(k, turn, sums, term=None, after=None, last=False):
        partner = partners[turn] if after is None else tie(partners[turn], after)
        return pair_solve(place, partner, mine[k], other[k], sums, term, tables, last, k == 1)

    terms = [None] * ROUNDS
    sums, terms[0] = pair(0, 0, None, after=partners[1][:3] + partners[2][:3])
    second = lax.all_to_all(tie(sets[1], terms[0]), "z", split_axis=0, concat_axis=0, tiled=True)
    sums, terms[1] = pair(0, 1, sums)
    sums, terms[2] = pair(0, 2, sums)
    mine.append(tie(second, terms[2]))
    other.append(swap(mine[1], "core", 1))
    sums, terms[3] = pair(0, 3, sums, last=True)
    back = [send_back(core_sum(*sums))]
    sums, cross = pair(1, 3, None, terms[3])
    handed = hand_over(cross)
    sums, side = pair(1, 1, sums, terms[1])
    sums, far = pair(1, 2, sums, terms[2], after=handed[2:])
    side = [side[0] + handed[0], side[1], side[2] + handed[2], side[3]]
    far = [far[0], far[1] + handed[1], far[2], far[3] + handed[3]]
    sent = swap(side[3], "band", 1)
    sums, own = pair(1, 0, sums, terms[0], after=[sent] + handed[:2], last=True)
    total = core_sum(*sums)
    back.append(send_back(total))
    arrived = [(swap(side[k], "band", 1), swap(far[k], "band", 2)) for k in range(PIECES - 1)]
    rest = own[3] + sent + swap(far[3], "band", 2)
    two = tie(own[2] + arrived[2][0] + arrived[2][1], total)
    return finish(back, scatter_line(own[0], own[1], two, rest, arrived[1], arrived[0]))


def solution(mesh):
    bands, planes = mesh.devices.shape
    inner = Mesh(mesh.devices.reshape(bands, planes // 2, 2), ("band", "z", "core"))
    placed = P("band", ("z", "core"), None)
    return jax.shard_map(local, mesh=inner, in_specs=(placed,), out_specs=placed, check_vma=False)
```

```python
import functools
import math

import jax
import jax.numpy as jnp
import numpy as np
from jax import lax
from jax.experimental import pallas as pl
from jax.experimental.pallas import tpu as pltpu
from jax.sharding import Mesh, PartitionSpec as P

PAIR = 2
ROUNDS = 4
OMEGA = 0.106
CELL = 41.05
ALPHA = 0.25
LANES = 128
F32 = jnp.float32
BF16 = jnp.bfloat16
MIDDLE = 12
GAP = 8
PIECES = 4


def hartley_table(count):
    index = np.arange(count)
    angle = (index[:, None] * index[None, :] % count).astype(np.float64) * (2.0 * math.pi / count)
    return (np.cos(angle) + np.sin(angle)).astype(np.float32)


def halves(value):
    high = value.astype(BF16)
    return high, (value - high.astype(F32)).astype(BF16)


def np_halves(value):
    high = value.astype(BF16)
    return high, (value - high.astype(np.float32)).astype(BF16)


def row_order(count):
    return np.arange(count).reshape(count // 4, 4).T.reshape(-1)


def lane_table(count):
    table = np.zeros((LANES, LANES), np.float32)
    table[:count, :count] = hartley_table(count)
    high, low = np_halves(table)
    top = np.concatenate([high, low], axis=1)
    return np.concatenate([top, np.concatenate([high, np.zeros_like(low)], axis=1)], axis=0)


def row_table(table):
    high, low = np_halves(table)
    top = np.concatenate([high, high], axis=1)
    return np.concatenate([top, np.concatenate([low, np.zeros_like(low)], axis=1)], axis=0)


def screened_kernel(count):
    shape = (count // 2, count, 2 * LANES)

    def squared(axis, place):
        index = place(lax.broadcasted_iota(jnp.int32, shape, axis))
        freq = jnp.where(index <= count // 2, index, index - count).astype(F32)
        return freq * freq

    second = 2 * lax.broadcasted_iota(jnp.int32, shape, 0)
    second = second + (lax.broadcasted_iota(jnp.int32, shape, 2) >= LANES).astype(jnp.int32)
    scale = (2.0 * math.pi / CELL) ** 2
    g_two = scale * (squared(0, lambda i: second) + squared(1, lambda i: i) + squared(2, lambda i: i % LANES))
    positive = g_two > 0
    safe = jnp.where(positive, g_two, 1.0)
    value = 4.0 * math.pi / safe * -jnp.expm1(-safe / (4.0 * OMEGA * OMEGA))
    value = jnp.where(positive, value, math.pi / (OMEGA * OMEGA))
    return value / float(count**3)


def to_rows(parts):
    first, second, third = parts
    lane = lax.broadcasted_iota(jnp.int32, first.shape, 1)
    row1 = jnp.where(lane < 32, pltpu.roll(first, 32, 1), pltpu.roll(second, 32, 1))
    row2 = jnp.where(lane < 64, pltpu.roll(second, 64, 1), pltpu.roll(third, 64, 1))
    row3 = pltpu.roll(third, 96, 1)
    return jnp.concatenate([first, row1, row2, row3], axis=0)


def from_rows(plane):
    step = plane.shape[0] // 4
    row0, row1, row2, row3 = (plane[k * step : (k + 1) * step] for k in range(4))
    lane = lax.broadcasted_iota(jnp.int32, row0.shape, 1)
    first = jnp.where(lane < 96, row0, pltpu.roll(row1, 96, 1))
    second = jnp.where(lane < 64, pltpu.roll(row1, 96, 1), pltpu.roll(row2, 64, 1))
    third = jnp.where(lane < 32, pltpu.roll(row2, 64, 1), pltpu.roll(row3, 32, 1))
    return first, second, third


def dot(a, b):
    return jnp.dot(a, b, preferred_element_type=F32)


def along_lanes(value, table):
    out = dot(jnp.concatenate(halves(value), axis=1), table)
    return out[:, :LANES] + out[:, LANES:]


def along_rows(table, value):
    out = dot(table, jnp.concatenate(halves(value), axis=0))
    half = out.shape[0] // 2
    return out[:half] + out[half:]


def pair_kernel(count, sizes, layout, *refs):
    split_in, sums_in, sums_split, terms_in, split_out = layout
    zs, planes = sizes
    slab = 2 * planes
    third, pitch = count // 4, count + GAP
    refs = list(refs)
    place = refs.pop(0)
    partner_hbm = [refs.pop(0) for _ in range(PIECES if split_in else 1)]
    mine_hbm, other_hbm = refs.pop(0), refs.pop(0)
    sums_hbm = refs.pop(0) if sums_in else None
    terms_hbm = refs.pop(0) if terms_in else None
    tables_hbm, coulomb_hbm = refs.pop(0), refs.pop(0)
    sums_out = [refs.pop(0) for _ in range(2 if sums_split else 1)]
    terms_out = [refs.pop(0) for _ in range(PIECES if split_out else 1)]
    partner, orbital, sums, terms, field, tables, coulomb, sem, sem_c = refs
    lanes = tables.at[: 2 * LANES]
    rows_in, rows_mid, rows_out = (
        tables.at[pl.ds(2 * LANES + 2 * count * k, 2 * count), : 2 * count] for k in range(3)
    )
    z, core = place[0], place[1]

    def part(ref, index, size=slab):
        return ref.at[pl.ds(pl.multiple_of(index * size, size), size)]

    def pieces(refs_):
        near = jnp.where(z == 0, 1, z - 1)
        return list(zip(refs_, [z, near, z ^ 2, 6 - z - near - (z ^ 2)]))

    def start(source, target, semaphore, there=None):
        def go():
            pltpu.make_async_copy(source, target, semaphore).start()

        if there is None:
            go()
        else:
            pl.when(there)(go)

    def wait(like_source, like_target, semaphore):
        pltpu.make_async_copy(like_source, like_target, semaphore).wait()

    start(tables_hbm, tables, sem_c.at[1])

    def load(s):
        if split_in:
            for ref, spot in pieces(partner_hbm):
                start(ref, part(partner, s), sem.at[0, s], spot == s)
        else:
            start(part(partner_hbm[0], s), part(partner, s), sem.at[0, s])
        start(mine_hbm.at[s], part(orbital, 2 * s + core, planes), sem.at[1, s])
        start(other_hbm.at[s], part(orbital, 2 * s + 1 - core, planes), sem.at[2, s])

    load(0)
    load(1)

    def density(x):
        parts = []
        for r in range(3):
            rows = pl.ds(r * third, third)
            parts.append(orbital[x, rows, :] * partner[x, rows, :])
        return to_rows(parts)

    group = planes

    def forward(step, carry):
        wait(part(partner, step), part(partner, step), sem.at[0, step])
        wait(part(orbital, 2 * step, planes), part(orbital, 2 * step, planes), sem.at[1, step])
        wait(part(orbital, 2 * step, planes), part(orbital, 2 * step, planes), sem.at[2, step])
        pl.when(step + 2 < zs)(lambda: load(step + 2))
        pl.when(step == zs - 2)(lambda: start(coulomb_hbm, coulomb, sem_c.at[0]))
        base = 2 * group * step
        pairs = [jnp.concatenate([density(base + 2 * g), density(base + 2 * g + 1)], axis=0) for g in range(group)]
        pairs = [along_lanes(both, lanes[...]) for both in pairs]
        pairs = [jnp.concatenate([both[:count], both[count:]], axis=1) for both in pairs]
        pairs = [along_rows(rows_in[...], both) for both in pairs]
        begin = pl.multiple_of(base * pitch, 2 * pitch)
        for g, both in enumerate(pairs):
            field[pl.ds(begin + 2 * g * pitch, count), :] = both[:, :LANES]
            field[pl.ds(begin + (2 * g + 1) * pitch, count), :] = both[:, LANES:]
        return carry

    wait(tables_hbm, tables, sem_c.at[1])
    lax.fori_loop(0, zs, forward, 0)
    for s in range(zs):
        if sums_in:
            start(part(sums_hbm, s), part(sums, s), sem.at[3, s])
        if terms_in:
            start(part(terms_hbm, s), part(terms, s), sem.at[4, s])
    wait(coulomb_hbm, coulomb, sem_c.at[0])

    def middle(step, carry):
        base = 2 * MIDDLE * step
        pairs = [
            jnp.concatenate(
                [field[pl.ds(base + 2 * g + k, count, stride=pitch), :] for k in range(2)], axis=1
            )
            for g in range(MIDDLE)
        ]
        pairs = [along_rows(rows_mid[...], both) for both in pairs]
        pairs = [both * coulomb[MIDDLE * step + g] for g, both in enumerate(pairs)]
        pairs = [along_rows(rows_mid[...], both) for both in pairs]
        for g, both in enumerate(pairs):
            for k in range(2):
                field[pl.ds(base + 2 * g + k, count, stride=pitch), :] = both[:, k * LANES : (k + 1) * LANES]
        return carry

    lax.fori_loop(0, count // 2 // MIDDLE, middle, 0)

    def backward(step, carry):
        if sums_in:
            wait(part(sums_hbm, step), part(sums, step), sem.at[3, step])
        if terms_in:
            wait(part(terms_hbm, step), part(terms, step), sem.at[4, step])
        base = 2 * group * step
        begin = pl.multiple_of(base * pitch, 2 * pitch)
        pairs = [
            jnp.concatenate([field[pl.ds(begin + (2 * g + k) * pitch, count), :] for k in range(2)], axis=1)
            for g in range(group)
        ]
        pairs = [along_rows(rows_out[...], both) for both in pairs]
        pairs = [jnp.concatenate([both[:, :LANES], both[:, LANES:]], axis=0) for both in pairs]
        pairs = [along_lanes(both, lanes[...]) for both in pairs]
        for g, both in enumerate(pairs):
            for k in range(2):
                x = base + 2 * g + k
                for r, value in enumerate(from_rows(both[k * count : (k + 1) * count])):
                    rows = pl.ds(r * third, third)
                    near = partner[x, rows, :] * value
                    sums[x, rows, :] = sums[x, rows, :] + near if sums_in else near
                    far = orbital[x, rows, :] * value
                    terms[x, rows, :] = terms[x, rows, :] + far if terms_in else far
        if sums_split:
            start(part(sums, 2 * step + core, planes), sums_out[0].at[step], sem.at[5, step])
            start(part(sums, 2 * step + 1 - core, planes), sums_out[1].at[step], sem.at[6, step])
        else:
            start(part(sums, step), part(sums_out[0], step), sem.at[5, step])
        if split_out:
            for ref, spot in pieces(terms_out):
                start(part(terms, step), ref, sem.at[7, step], spot == step)
        else:
            start(part(terms, step), part(terms_out[0], step), sem.at[7, step])
        return carry

    lax.fori_loop(0, zs, backward, 0)
    for s in range(zs):
        if sums_split:
            for k in range(2):
                wait(part(sums, s, planes), sums_out[k].at[s], sem.at[5 + k, s])
        else:
            wait(part(sums, s), part(sums_out[0], s), sem.at[5, s])
        target = terms_out[0] if split_out else part(terms_out[0], s)
        wait(part(terms, s), target, sem.at[7, s])


def pair_solve(place, partner, mine, other, sums, terms, tables, last_partner, last_orbital):
    zs, planes, rows, _ = mine.shape
    count = zs * 2 * planes
    split_in = len(partner) > 1
    layout = (split_in, sums is not None, last_partner, terms is not None, last_orbital and split_in)
    field = jax.ShapeDtypeStruct((count, rows, LANES), F32)
    kinds = [jax.ShapeDtypeStruct(mine.shape, F32)] * 2 if last_partner else [field]
    pieces = [jax.ShapeDtypeStruct(p.shape, F32) for p in partner] if layout[4] else [field]
    more = [a for a in (sums, terms) if a is not None]
    anywhere = pl.BlockSpec(memory_space=pl.ANY)
    block = (count, rows, LANES)
    out = pl.pallas_call(
        functools.partial(pair_kernel, count, (zs, planes), layout),
        in_specs=[pl.BlockSpec(memory_space=pltpu.SMEM)]
        + [anywhere] * (len(partner) + 4 + len(more)),
        out_specs=[anywhere] * (len(kinds) + len(pieces)),
        out_shape=kinds + pieces,
        scratch_shapes=[pltpu.VMEM(block, F32)] * 4
        + [
            pltpu.VMEM((count * (count + GAP), LANES), F32),
            pltpu.VMEM(tables[0].shape, BF16),
            pltpu.VMEM(tables[1].shape, F32),
            pltpu.SemaphoreType.DMA((8, zs)),
            pltpu.SemaphoreType.DMA((2,)),
        ],
        cost_estimate=pl.CostEstimate(
            flops=200 * count**4, bytes_accessed=20 * count * rows * LANES, transcendentals=0
        ),
        compiler_params=pltpu.CompilerParams(vmem_limit_bytes=60 * 1024 * 1024),
    )(place, *partner, mine, other, *more, *tables)
    sums = out[:2] if last_partner else out[0]
    terms = out[len(kinds) :] if layout[4] else out[-1]
    return sums, terms


def make_tables(count):
    table = hartley_table(count)
    order = row_order(count)
    rows = [row_table(t) for t in (table[:, order], table, table[order, :])]
    rows = [np.pad(t, ((0, 0), (0, 2 * LANES - t.shape[1]))) for t in rows]
    return jnp.asarray(np.concatenate([lane_table(count)] + rows, axis=0)), screened_kernel(count)


def piece_row(tile, rows):
    return tile % 3 * (rows // 3) + tile // 3


def pack_kernel(sets, planes, rows, flat, *packed):
    size = flat.shape[1] // sets
    plane = pl.program_id(0)
    for tile in range(rows):
        row = plane * rows + piece_row(tile, rows)
        for k in range(sets):
            value = flat[0, k * size : (k + 1) * size, tile * LANES : (tile + 1) * LANES]
            packed[k][pl.ds(row, size, stride=planes * rows), :] = value


def pack(fields, sets):
    planes, number, flat = fields.shape
    rows, size = flat // LANES, number // sets
    out = (size * planes * rows, LANES)
    packed = pl.pallas_call(
        functools.partial(pack_kernel, sets, planes, rows),
        grid=(planes,),
        in_specs=[pl.BlockSpec((1, number, flat), lambda i: (i, 0, 0))],
        out_specs=[pl.BlockSpec(out, lambda i: (0, 0))] * sets,
        out_shape=[jax.ShapeDtypeStruct(out, F32)] * sets,
        compiler_params=pltpu.CompilerParams(vmem_limit_bytes=32 * 1024 * 1024),
    )(fields)
    return [p.reshape(size, planes, rows, LANES) for p in packed]


def unpack_kernel(sets, planes, rows, *refs):
    packed, extra, flat = refs[:sets], refs[sets], refs[-1]
    size = flat.shape[1] // sets
    plane = pl.program_id(0)
    for tile in range(rows):
        row = plane * rows + piece_row(tile, rows)
        more = extra[pl.ds(row, PAIR, stride=planes * rows), :]
        for k in range(sets):
            value = packed[k][pl.ds(row, size, stride=planes * rows), :]
            if k == 0:
                value = jnp.concatenate([value[:PAIR] + more, value[PAIR:]], axis=0)
            flat[0, k * size : (k + 1) * size, tile * LANES : (tile + 1) * LANES] = -ALPHA * value


def unpack(fields, extra):
    sets = len(fields)
    size, planes, rows, _ = fields[0].shape
    whole = lambda n: pl.BlockSpec((n * planes * rows, LANES), lambda i: (0, 0), pipeline_mode=pl.Buffered(1))
    return pl.pallas_call(
        functools.partial(unpack_kernel, sets, planes, rows),
        grid=(planes,),
        in_specs=[whole(size)] * sets + [whole(PAIR)],
        out_specs=pl.BlockSpec((1, sets * size, rows * LANES), lambda i: (i, 0, 0)),
        out_shape=jax.ShapeDtypeStruct((planes, sets * size, rows * LANES), F32),
        compiler_params=pltpu.CompilerParams(vmem_limit_bytes=32 * 1024 * 1024),
    )(*(f.reshape(size * planes * rows, LANES) for f in fields), extra.reshape(PAIR * planes * rows, LANES))


def swap(value, axis, flip):
    size = lax.axis_size(axis)
    return lax.ppermute(value, axis, [(i, i ^ flip) for i in range(size)])


def along(value, pairs):
    return lax.ppermute(value, "z", pairs)


def tie(values, done):
    return lax.optimization_barrier((values, done))[0]


RIGHT = [(0, 1), (1, 2), (2, 3)]
LEFT = [(1, 0), (2, 1), (3, 2)]


def spread(slab, first):
    z = lax.axis_index("z")
    side, far = [], []

    def both(piece):
        side.append(swap(piece, "band", 1))
        far.append(swap(piece, "band", 2))

    before, after = along(slab, RIGHT), along(slab, LEFT)
    both(slab)
    cross = [swap(side[0], "band", 2)]
    before, after = tie((before, after), (side[-1], far[-1], first, cross))
    near = jnp.where(z == 0, after, before)
    two = along(before, RIGHT[1:]) + along(after, LEFT[:2])
    both(near)
    two = tie(two, (side[-1], far[-1]))
    both(two)
    rest = jnp.where((z == 0) | (z == 3), along(two, [(2, 3), (1, 0)]), after)
    rest = tie(rest, (side[-1], far[-1]))
    both(rest)
    done = (side[3], far[3])
    cross += [swap(tie(far[1], done), "band", 1), swap(tie(side[2], done), "band", 2)]
    cross.append(swap(tie(far[3], cross[1]), "band", 1))
    return [[slab, near, two, rest], side, far, cross]


def local(orbitals):
    n_local, planes, flat = orbitals.shape
    zs, bands, core = lax.axis_size("z"), lax.axis_size("band"), lax.axis_index("core")
    count = planes * zs * 2
    place = jnp.stack([lax.axis_index("z"), core]).astype(jnp.int32)
    tables = make_tables(count)
    sets = pack(orbitals.swapaxes(0, 1), n_local // zs)
    tail = sets[0].shape[2:]
    keep = lax.dynamic_index_in_dim(sets[0], core, 0, keepdims=False)
    come = swap(lax.dynamic_index_in_dim(sets[0], 1 - core, 0, keepdims=False), "core", 1)
    slab = jnp.concatenate([jnp.where(core == 0, keep, come), jnp.where(core == 0, come, keep)], axis=0)
    square = bands == ROUNDS == 4 and zs == 4 and len(sets) == 2
    if square:
        return square_local(place, tables, sets, slab)
    every = lax.all_gather(slab, ("band", "z"), axis=0, tiled=True).reshape((bands, count) + tail)
    terms = [None] * ROUNDS
    sums_out = []
    for k, fields in enumerate(sets):
        mine = lax.all_to_all(fields, "z", split_axis=0, concat_axis=0, tiled=True)
        other = swap(mine, "core", 1)
        sums = None
        for turn in range(ROUNDS):
            sums, terms[turn] = pair_solve(
                place, [every[turn]], mine, other, sums, terms[turn], tables, turn == ROUNDS - 1, k == len(sets) - 1
            )
        sums_out.append(sums)
    owner = jnp.concatenate([t[None] for t in terms] + [jnp.zeros((bands - ROUNDS, count) + tail, F32)], axis=0)
    owner = owner.reshape((bands * count,) + tail)
    owner = lax.psum_scatter(owner, ("band", "z"), scatter_dimension=0, tiled=True)
    return finish([send_back(core_sum(*sums)) for sums in sums_out], owner)


def core_sum(keep, give):
    return keep + swap(give, "core", 1)


def send_back(total):
    return lax.all_to_all(total, "z", split_axis=0, concat_axis=0, tiled=True)


def finish(sums, owner):
    core, planes = lax.axis_index("core"), owner.shape[0] // 2
    keep = lax.dynamic_slice_in_dim(owner, core * planes, planes)
    come = swap(lax.dynamic_slice_in_dim(owner, (1 - core) * planes, planes), "core", 1)
    owner = jnp.stack([jnp.where(core == 0, keep, come), jnp.where(core == 0, come, keep)])
    return unpack(sums, owner).swapaxes(0, 1)


def square_local(place, tables, sets, slab):
    first = lax.all_to_all(sets[0], "z", split_axis=0, concat_axis=0, tiled=True)
    partners = spread(slab, first)
    mine, other = [first], [swap(first, "core", 1)]

    def pair(k, turn, sums, term=None, after=None, last=False):
        partner = partners[turn] if after is None else tie(partners[turn], after)
        return pair_solve(place, partner, mine[k], other[k], sums, term, tables, last, k == 1)

    terms = [None] * ROUNDS
    sums, terms[0] = pair(0, 0, None)
    second = lax.all_to_all(tie(sets[1], partners[0][3]), "z", split_axis=0, concat_axis=0, tiled=True)
    sums, terms[1] = pair(0, 1, sums)
    sums, terms[2] = pair(0, 2, sums, after=partners[3][:3])
    sums, terms[3] = pair(0, 3, sums, last=True)
    mine.append(tie(second, terms[3]))
    other.append(swap(mine[1], "core", 1))
    back = [send_back(core_sum(*sums))]
    z = lax.axis_index("z")
    x_swap = lambda value, done: swap(tie(value, done), "band", 1)
    y_swap = lambda value, done: swap(tie(value, done), "band", 2)
    sums, cross = pair(1, 3, None, terms[3])
    handed3, handed2 = swap(cross[3], "band", 1), swap(cross[2], "band", 2)
    sums, side = pair(1, 1, sums, terms[1])
    done = (handed3, handed2)
    side3, handed0 = x_swap(side[3], done), y_swap(cross[0], done)
    sums, far = pair(1, 2, sums, terms[2], after=done)
    done = (side3, handed0)
    side2, far3 = x_swap(side[2] + handed2, done), y_swap(far[3] + handed3, done)
    sums, own = pair(1, 0, sums, terms[0], after=done, last=True)
    total = core_sum(*sums)
    back.append(send_back(total))
    done = (side2, far3)
    handed1, far2 = x_swap(cross[1], done), y_swap(far[2], done)
    rest = along(own[3] + side3 + far3, [(0, 1), (3, 2)])
    done = (handed1, far2)
    side1, far1 = x_swap(side[1], done), y_swap(far[1] + handed1, done)
    two = tie(own[2] + side2 + far2 + rest, total)
    after, before = along(two, RIGHT[:2]), along(two, LEFT[1:])
    done = (side1, far1)
    side0, far0 = x_swap(side[0] + handed0, done), y_swap(far[0], done)
    near = own[1] + side1 + far1
    after = jnp.where(z == 0, near, own[3] + side3 + far3 + after)
    after, before = along(after, RIGHT), along(near + before, LEFT)
    return finish(back, own[0] + side0 + far0 + after + before)


def solution(mesh):
    bands, planes = mesh.devices.shape
    inner = Mesh(mesh.devices.reshape(bands, planes // 2, 2), ("band", "z", "core"))
    placed = P("band", ("z", "core"), None)
    return jax.shard_map(local, mesh=inner, in_specs=(placed,), out_specs=placed, check_vma=False)
```

```python
import functools
import math

import jax
import jax.numpy as jnp
import numpy as np
from jax import lax
from jax.experimental import pallas as pl
from jax.experimental.pallas import tpu as pltpu
from jax.sharding import Mesh, PartitionSpec as P

PAIR = 2
ROUNDS = 4
OMEGA = 0.106
CELL = 41.05
ALPHA = 0.25
LANES = 128
F32 = jnp.float32
BF16 = jnp.bfloat16
MIDDLE = 12
GAP = 8
PIECES = 4


def hartley_table(count):
    index = np.arange(count)
    angle = (index[:, None] * index[None, :] % count).astype(np.float64) * (2.0 * math.pi / count)
    return (np.cos(angle) + np.sin(angle)).astype(np.float32)


def halves(value):
    high = value.astype(BF16)
    return high, (value - high.astype(F32)).astype(BF16)


def np_halves(value):
    high = value.astype(BF16)
    return high, (value - high.astype(np.float32)).astype(BF16)


def row_order(count):
    return np.arange(count).reshape(count // 4, 4).T.reshape(-1)


def lane_table(count):
    table = np.zeros((LANES, LANES), np.float32)
    table[:count, :count] = hartley_table(count)
    high, low = np_halves(table)
    top = np.concatenate([high, low], axis=1)
    return np.concatenate([top, np.concatenate([high, np.zeros_like(low)], axis=1)], axis=0)


def row_table(table):
    high, low = np_halves(table)
    top = np.concatenate([high, high], axis=1)
    return np.concatenate([top, np.concatenate([low, np.zeros_like(low)], axis=1)], axis=0)


def screened_kernel(count):
    shape = (count // 2, count, 2 * LANES)

    def squared(axis, place):
        index = place(lax.broadcasted_iota(jnp.int32, shape, axis))
        freq = jnp.where(index <= count // 2, index, index - count).astype(F32)
        return freq * freq

    second = 2 * lax.broadcasted_iota(jnp.int32, shape, 0)
    second = second + (lax.broadcasted_iota(jnp.int32, shape, 2) >= LANES).astype(jnp.int32)
    scale = (2.0 * math.pi / CELL) ** 2
    g_two = scale * (squared(0, lambda i: second) + squared(1, lambda i: i) + squared(2, lambda i: i % LANES))
    positive = g_two > 0
    safe = jnp.where(positive, g_two, 1.0)
    value = 4.0 * math.pi / safe * -jnp.expm1(-safe / (4.0 * OMEGA * OMEGA))
    value = jnp.where(positive, value, math.pi / (OMEGA * OMEGA))
    return value / float(count**3)


def to_rows(parts):
    first, second, third = parts
    lane = lax.broadcasted_iota(jnp.int32, first.shape, 1)
    row1 = jnp.where(lane < 32, pltpu.roll(first, 32, 1), pltpu.roll(second, 32, 1))
    row2 = jnp.where(lane < 64, pltpu.roll(second, 64, 1), pltpu.roll(third, 64, 1))
    row3 = pltpu.roll(third, 96, 1)
    return jnp.concatenate([first, row1, row2, row3], axis=0)


def from_rows(plane):
    step = plane.shape[0] // 4
    row0, row1, row2, row3 = (plane[k * step : (k + 1) * step] for k in range(4))
    lane = lax.broadcasted_iota(jnp.int32, row0.shape, 1)
    first = jnp.where(lane < 96, row0, pltpu.roll(row1, 96, 1))
    second = jnp.where(lane < 64, pltpu.roll(row1, 96, 1), pltpu.roll(row2, 64, 1))
    third = jnp.where(lane < 32, pltpu.roll(row2, 64, 1), pltpu.roll(row3, 32, 1))
    return first, second, third


def dot(a, b):
    return jnp.dot(a, b, preferred_element_type=F32)


def along_lanes(value, table):
    out = dot(jnp.concatenate(halves(value), axis=1), table)
    return out[:, :LANES] + out[:, LANES:]


def along_rows(table, value):
    out = dot(table, jnp.concatenate(halves(value), axis=0))
    half = out.shape[0] // 2
    return out[:half] + out[half:]


def pair_kernel(count, sizes, layout, *refs):
    split_in, sums_in, sums_split, terms_in, split_out = layout
    zs, planes = sizes
    slab = 2 * planes
    third, pitch = count // 4, count + GAP
    refs = list(refs)
    place = refs.pop(0)
    partner_hbm = [refs.pop(0) for _ in range(PIECES if split_in else 1)]
    mine_hbm, other_hbm = refs.pop(0), refs.pop(0)
    sums_hbm = refs.pop(0) if sums_in else None
    terms_hbm = refs.pop(0) if terms_in else None
    tables_hbm, coulomb_hbm = refs.pop(0), refs.pop(0)
    sums_out = [refs.pop(0) for _ in range(2 if sums_split else 1)]
    terms_out = [refs.pop(0) for _ in range(PIECES if split_out else 1)]
    partner, orbital, sums, terms, field, tables, coulomb, sem, sem_c = refs
    lanes = tables.at[: 2 * LANES]
    rows_in, rows_mid, rows_out = (
        tables.at[pl.ds(2 * LANES + 2 * count * k, 2 * count), : 2 * count] for k in range(3)
    )
    z, core = place[0], place[1]

    def part(ref, index, size=slab):
        return ref.at[pl.ds(pl.multiple_of(index * size, size), size)]

    def pieces(refs_):
        near = jnp.where(z == 0, 1, z - 1)
        return list(zip(refs_, [z, near, z ^ 2, 6 - z - near - (z ^ 2)]))

    def start(source, target, semaphore, there=None):
        def go():
            pltpu.make_async_copy(source, target, semaphore).start()

        if there is None:
            go()
        else:
            pl.when(there)(go)

    def wait(like_source, like_target, semaphore):
        pltpu.make_async_copy(like_source, like_target, semaphore).wait()

    start(tables_hbm, tables, sem_c.at[1])

    def load(s):
        if split_in:
            for ref, spot in pieces(partner_hbm):
                start(ref, part(partner, s), sem.at[0, s], spot == s)
        else:
            start(part(partner_hbm[0], s), part(partner, s), sem.at[0, s])
        start(mine_hbm.at[s], part(orbital, 2 * s + core, planes), sem.at[1, s])
        start(other_hbm.at[s], part(orbital, 2 * s + 1 - core, planes), sem.at[2, s])

    load(0)
    load(1)

    def density(x):
        parts = []
        for r in range(3):
            rows = pl.ds(r * third, third)
            parts.append(orbital[x, rows, :] * partner[x, rows, :])
        return to_rows(parts)

    group = planes

    def forward(step, carry):
        wait(part(partner, step), part(partner, step), sem.at[0, step])
        wait(part(orbital, 2 * step, planes), part(orbital, 2 * step, planes), sem.at[1, step])
        wait(part(orbital, 2 * step, planes), part(orbital, 2 * step, planes), sem.at[2, step])
        pl.when(step + 2 < zs)(lambda: load(step + 2))
        pl.when(step == zs - 2)(lambda: start(coulomb_hbm, coulomb, sem_c.at[0]))
        base = 2 * group * step
        pairs = [jnp.concatenate([density(base + 2 * g), density(base + 2 * g + 1)], axis=0) for g in range(group)]
        pairs = [along_lanes(both, lanes[...]) for both in pairs]
        pairs = [jnp.concatenate([both[:count], both[count:]], axis=1) for both in pairs]
        pairs = [along_rows(rows_in[...], both) for both in pairs]
        begin = pl.multiple_of(base * pitch, 2 * pitch)
        for g, both in enumerate(pairs):
            field[pl.ds(begin + 2 * g * pitch, count), :] = both[:, :LANES]
            field[pl.ds(begin + (2 * g + 1) * pitch, count), :] = both[:, LANES:]
        return carry

    wait(tables_hbm, tables, sem_c.at[1])
    lax.fori_loop(0, zs, forward, 0)
    for s in range(zs):
        if sums_in:
            start(part(sums_hbm, s), part(sums, s), sem.at[3, s])
        if terms_in:
            start(part(terms_hbm, s), part(terms, s), sem.at[4, s])
    wait(coulomb_hbm, coulomb, sem_c.at[0])

    def middle(step, carry):
        base = 2 * MIDDLE * step
        pairs = [
            jnp.concatenate(
                [field[pl.ds(base + 2 * g + k, count, stride=pitch), :] for k in range(2)], axis=1
            )
            for g in range(MIDDLE)
        ]
        pairs = [along_rows(rows_mid[...], both) for both in pairs]
        pairs = [both * coulomb[MIDDLE * step + g] for g, both in enumerate(pairs)]
        pairs = [along_rows(rows_mid[...], both) for both in pairs]
        for g, both in enumerate(pairs):
            for k in range(2):
                field[pl.ds(base + 2 * g + k, count, stride=pitch), :] = both[:, k * LANES : (k + 1) * LANES]
        return carry

    lax.fori_loop(0, count // 2 // MIDDLE, middle, 0)

    def backward(step, carry):
        if sums_in:
            wait(part(sums_hbm, step), part(sums, step), sem.at[3, step])
        if terms_in:
            wait(part(terms_hbm, step), part(terms, step), sem.at[4, step])
        base = 2 * group * step
        begin = pl.multiple_of(base * pitch, 2 * pitch)
        pairs = [
            jnp.concatenate([field[pl.ds(begin + (2 * g + k) * pitch, count), :] for k in range(2)], axis=1)
            for g in range(group)
        ]
        pairs = [along_rows(rows_out[...], both) for both in pairs]
        pairs = [jnp.concatenate([both[:, :LANES], both[:, LANES:]], axis=0) for both in pairs]
        pairs = [along_lanes(both, lanes[...]) for both in pairs]
        for g, both in enumerate(pairs):
            for k in range(2):
                x = base + 2 * g + k
                for r, value in enumerate(from_rows(both[k * count : (k + 1) * count])):
                    rows = pl.ds(r * third, third)
                    near = partner[x, rows, :] * value
                    sums[x, rows, :] = sums[x, rows, :] + near if sums_in else near
                    far = orbital[x, rows, :] * value
                    terms[x, rows, :] = terms[x, rows, :] + far if terms_in else far
        if sums_split:
            start(part(sums, 2 * step + core, planes), sums_out[0].at[step], sem.at[5, step])
            start(part(sums, 2 * step + 1 - core, planes), sums_out[1].at[step], sem.at[6, step])
        else:
            start(part(sums, step), part(sums_out[0], step), sem.at[5, step])
        if split_out:
            for ref, spot in pieces(terms_out):
                start(part(terms, step), ref, sem.at[7, step], spot == step)
        else:
            start(part(terms, step), part(terms_out[0], step), sem.at[7, step])
        return carry

    lax.fori_loop(0, zs, backward, 0)
    for s in range(zs):
        if sums_split:
            for k in range(2):
                wait(part(sums, s, planes), sums_out[k].at[s], sem.at[5 + k, s])
        else:
            wait(part(sums, s), part(sums_out[0], s), sem.at[5, s])
        target = terms_out[0] if split_out else part(terms_out[0], s)
        wait(part(terms, s), target, sem.at[7, s])


def pair_solve(place, partner, mine, other, sums, terms, tables, last_partner, last_orbital):
    zs, planes, rows, _ = mine.shape
    count = zs * 2 * planes
    split_in = len(partner) > 1
    layout = (split_in, sums is not None, last_partner, terms is not None, last_orbital and split_in)
    field = jax.ShapeDtypeStruct((count, rows, LANES), F32)
    kinds = [jax.ShapeDtypeStruct(mine.shape, F32)] * 2 if last_partner else [field]
    pieces = [jax.ShapeDtypeStruct(p.shape, F32) for p in partner] if layout[4] else [field]
    more = [a for a in (sums, terms) if a is not None]
    anywhere = pl.BlockSpec(memory_space=pl.ANY)
    block = (count, rows, LANES)
    out = pl.pallas_call(
        functools.partial(pair_kernel, count, (zs, planes), layout),
        in_specs=[pl.BlockSpec(memory_space=pltpu.SMEM)]
        + [anywhere] * (len(partner) + 4 + len(more)),
        out_specs=[anywhere] * (len(kinds) + len(pieces)),
        out_shape=kinds + pieces,
        scratch_shapes=[pltpu.VMEM(block, F32)] * 4
        + [
            pltpu.VMEM((count * (count + GAP), LANES), F32),
            pltpu.VMEM(tables[0].shape, BF16),
            pltpu.VMEM(tables[1].shape, F32),
            pltpu.SemaphoreType.DMA((8, zs)),
            pltpu.SemaphoreType.DMA((2,)),
        ],
        cost_estimate=pl.CostEstimate(
            flops=200 * count**4, bytes_accessed=20 * count * rows * LANES, transcendentals=0
        ),
        compiler_params=pltpu.CompilerParams(vmem_limit_bytes=60 * 1024 * 1024),
    )(place, *partner, mine, other, *more, *tables)
    sums = out[:2] if last_partner else out[0]
    terms = out[len(kinds) :] if layout[4] else out[-1]
    return sums, terms


def make_tables(count):
    table = hartley_table(count)
    order = row_order(count)
    rows = [row_table(t) for t in (table[:, order], table, table[order, :])]
    rows = [np.pad(t, ((0, 0), (0, 2 * LANES - t.shape[1]))) for t in rows]
    return jnp.asarray(np.concatenate([lane_table(count)] + rows, axis=0)), screened_kernel(count)


def piece_row(tile, rows):
    return tile % 3 * (rows // 3) + tile // 3


def pack_kernel(sets, planes, rows, flat, *packed):
    size = flat.shape[1] // sets
    plane = pl.program_id(0)
    for tile in range(rows):
        row = plane * rows + piece_row(tile, rows)
        for k in range(sets):
            value = flat[0, k * size : (k + 1) * size, tile * LANES : (tile + 1) * LANES]
            packed[k][pl.ds(row, size, stride=planes * rows), :] = value


def pack(fields, sets):
    planes, number, flat = fields.shape
    rows, size = flat // LANES, number // sets
    out = (size * planes * rows, LANES)
    packed = pl.pallas_call(
        functools.partial(pack_kernel, sets, planes, rows),
        grid=(planes,),
        in_specs=[pl.BlockSpec((1, number, flat), lambda i: (i, 0, 0))],
        out_specs=[pl.BlockSpec(out, lambda i: (0, 0))] * sets,
        out_shape=[jax.ShapeDtypeStruct(out, F32)] * sets,
        compiler_params=pltpu.CompilerParams(vmem_limit_bytes=32 * 1024 * 1024),
    )(fields)
    return [p.reshape(size, planes, rows, LANES) for p in packed]


def unpack_kernel(sets, planes, rows, *refs):
    packed, extra, flat = refs[:sets], refs[sets], refs[-1]
    size = flat.shape[1] // sets
    plane = pl.program_id(0)
    for tile in range(rows):
        row = plane * rows + piece_row(tile, rows)
        more = extra[pl.ds(row, PAIR, stride=planes * rows), :]
        for k in range(sets):
            value = packed[k][pl.ds(row, size, stride=planes * rows), :]
            if k == 0:
                value = jnp.concatenate([value[:PAIR] + more, value[PAIR:]], axis=0)
            flat[0, k * size : (k + 1) * size, tile * LANES : (tile + 1) * LANES] = -ALPHA * value


def unpack(fields, extra):
    sets = len(fields)
    size, planes, rows, _ = fields[0].shape
    whole = lambda n: pl.BlockSpec((n * planes * rows, LANES), lambda i: (0, 0), pipeline_mode=pl.Buffered(1))
    return pl.pallas_call(
        functools.partial(unpack_kernel, sets, planes, rows),
        grid=(planes,),
        in_specs=[whole(size)] * sets + [whole(PAIR)],
        out_specs=pl.BlockSpec((1, sets * size, rows * LANES), lambda i: (i, 0, 0)),
        out_shape=jax.ShapeDtypeStruct((planes, sets * size, rows * LANES), F32),
        compiler_params=pltpu.CompilerParams(vmem_limit_bytes=32 * 1024 * 1024),
    )(*(f.reshape(size * planes * rows, LANES) for f in fields), extra.reshape(PAIR * planes * rows, LANES))


def swap(value, axis, flip):
    size = lax.axis_size(axis)
    return lax.ppermute(value, axis, [(i, i ^ flip) for i in range(size)])


def along(value, pairs):
    return lax.ppermute(value, "z", pairs)


def tie(values, done):
    return lax.optimization_barrier((values, done))[0]


RIGHT = [(0, 1), (1, 2), (2, 3)]
LEFT = [(1, 0), (2, 1), (3, 2)]


def spread(slab, first):
    z = lax.axis_index("z")
    side, far = [], []

    def both(piece):
        side.append(swap(piece, "band", 1))
        far.append(swap(piece, "band", 2))

    before, after = along(slab, RIGHT), along(slab, LEFT)
    both(slab)
    cross = [swap(side[0], "band", 2)]
    before, after = tie((before, after), (side[-1], far[-1], first, cross))
    near = jnp.where(z == 0, after, before)
    two = along(before, RIGHT[1:]) + along(after, LEFT[:2])
    both(near)
    two = tie(two, (side[-1], far[-1]))
    both(two)
    rest = jnp.where((z == 0) | (z == 3), along(two, [(2, 3), (1, 0)]), after)
    rest = tie(rest, (side[-1], far[-1]))
    both(rest)
    done = (side[3], far[3])
    cross += [swap(tie(far[1], done), "band", 1), swap(tie(side[2], done), "band", 2)]
    cross.append(swap(tie(far[3], cross[1]), "band", 1))
    return [[slab, near, two, rest], side, far, cross]


def local(orbitals):
    n_local, planes, flat = orbitals.shape
    zs, bands, core = lax.axis_size("z"), lax.axis_size("band"), lax.axis_index("core")
    count = planes * zs * 2
    place = jnp.stack([lax.axis_index("z"), core]).astype(jnp.int32)
    tables = make_tables(count)
    sets = pack(orbitals.swapaxes(0, 1), n_local // zs)
    tail = sets[0].shape[2:]
    keep = lax.dynamic_index_in_dim(sets[0], core, 0, keepdims=False)
    come = swap(lax.dynamic_index_in_dim(sets[0], 1 - core, 0, keepdims=False), "core", 1)
    slab = jnp.concatenate([jnp.where(core == 0, keep, come), jnp.where(core == 0, come, keep)], axis=0)
    square = bands == ROUNDS == 4 and zs == 4 and len(sets) == 2
    if square:
        return square_local(place, tables, sets, slab)
    every = lax.all_gather(slab, ("band", "z"), axis=0, tiled=True).reshape((bands, count) + tail)
    terms = [None] * ROUNDS
    sums_out = []
    for k, fields in enumerate(sets):
        mine = lax.all_to_all(fields, "z", split_axis=0, concat_axis=0, tiled=True)
        other = swap(mine, "core", 1)
        sums = None
        for turn in range(ROUNDS):
            sums, terms[turn] = pair_solve(
                place, [every[turn]], mine, other, sums, terms[turn], tables, turn == ROUNDS - 1, k == len(sets) - 1
            )
        sums_out.append(sums)
    owner = jnp.concatenate([t[None] for t in terms] + [jnp.zeros((bands - ROUNDS, count) + tail, F32)], axis=0)
    owner = owner.reshape((bands * count,) + tail)
    owner = lax.psum_scatter(owner, ("band", "z"), scatter_dimension=0, tiled=True)
    return finish([send_back(core_sum(*sums)) for sums in sums_out], owner)


def core_sum(keep, give):
    return keep + swap(give, "core", 1)


def send_back(total):
    return lax.all_to_all(total, "z", split_axis=0, concat_axis=0, tiled=True)


def finish(sums, owner):
    core, planes = lax.axis_index("core"), owner.shape[0] // 2
    keep = lax.dynamic_slice_in_dim(owner, core * planes, planes)
    come = swap(lax.dynamic_slice_in_dim(owner, (1 - core) * planes, planes), "core", 1)
    owner = jnp.stack([jnp.where(core == 0, keep, come), jnp.where(core == 0, come, keep)])
    return unpack(sums, owner).swapaxes(0, 1)


def square_local(place, tables, sets, slab):
    first = lax.all_to_all(sets[0], "z", split_axis=0, concat_axis=0, tiled=True)
    partners = spread(slab, first)
    mine, other = [first], [swap(first, "core", 1)]

    def pair(k, turn, sums, term=None, after=None, last=False):
        partner = partners[turn] if after is None else tie(partners[turn], after)
        return pair_solve(place, partner, mine[k], other[k], sums, term, tables, last, k == 1)

    terms = [None] * ROUNDS
    sums, terms[0] = pair(0, 0, None)
    second = lax.all_to_all(tie(sets[1], partners[0][3]), "z", split_axis=0, concat_axis=0, tiled=True)
    sums, terms[1] = pair(0, 1, sums)
    sums, terms[2] = pair(0, 2, sums, after=partners[3][:3])
    sums, terms[3] = pair(0, 3, sums, last=True)
    mine.append(tie(second, terms[3]))
    other.append(swap(mine[1], "core", 1))
    back = [send_back(core_sum(*sums))]
    z = lax.axis_index("z")
    x_swap = lambda value, done: swap(tie(value, done), "band", 1)
    y_swap = lambda value, done: swap(tie(value, done), "band", 2)
    sums, cross = pair(1, 3, None, terms[3])
    handed3, handed2 = swap(cross[3], "band", 1), swap(cross[2], "band", 2)
    sums, side = pair(1, 1, sums, terms[1])
    done = (handed3, handed2)
    side3, handed0 = x_swap(side[3], done), y_swap(cross[0], done)
    sums, far = pair(1, 2, sums, terms[2], after=done)
    done = (side3, handed0)
    side2, far3 = x_swap(side[2] + handed2, done), y_swap(far[3] + handed3, done)
    sums, own = pair(1, 0, sums, terms[0], after=done + (back[0],), last=True)
    total = core_sum(*sums)
    back.append(send_back(total))
    done = (side2, far3)
    handed1, far2 = x_swap(cross[1], done), y_swap(far[2], done)
    rest = along(own[3] + side3 + far3, [(0, 1), (3, 2)])
    done = (handed1, far2)
    side1, far1 = x_swap(side[1], done), y_swap(far[1] + handed1, done)
    two = tie(own[2] + side2 + far2 + rest, total)
    after, before = along(two, RIGHT[:2]), along(two, LEFT[1:])
    done = (side1, far1)
    side0, far0 = x_swap(side[0] + handed0, done), y_swap(far[0], done)
    near = own[1] + side1 + far1
    after = jnp.where(z == 0, near, own[3] + side3 + far3 + after)
    after, before = along(after, RIGHT), along(near + before, LEFT)
    return finish(back, own[0] + side0 + far0 + after + before)


def solution(mesh):
    bands, planes = mesh.devices.shape
    inner = Mesh(mesh.devices.reshape(bands, planes // 2, 2), ("band", "z", "core"))
    placed = P("band", ("z", "core"), None)
    return jax.shard_map(local, mesh=inner, in_specs=(placed,), out_specs=placed, check_vma=False)
```

```python
import functools
import math

import jax
import jax.numpy as jnp
import numpy as np
from jax import lax
from jax.experimental import pallas as pl
from jax.experimental.pallas import tpu as pltpu
from jax.sharding import Mesh, PartitionSpec as P

PAIR = 2
ROUNDS = 4
OMEGA = 0.106
CELL = 41.05
ALPHA = 0.25
LANES = 128
F32 = jnp.float32
BF16 = jnp.bfloat16
MIDDLE = 12
GAP = 8
PIECES = 4


def hartley_table(count):
    index = np.arange(count)
    angle = (index[:, None] * index[None, :] % count).astype(np.float64) * (2.0 * math.pi / count)
    return (np.cos(angle) + np.sin(angle)).astype(np.float32)


def halves(value):
    high = value.astype(BF16)
    return high, (value - high.astype(F32)).astype(BF16)


def np_halves(value):
    high = value.astype(BF16)
    return high, (value - high.astype(np.float32)).astype(BF16)


def row_order(count):
    return np.arange(count).reshape(count // 4, 4).T.reshape(-1)


def lane_table(count):
    table = np.zeros((LANES, LANES), np.float32)
    table[:count, :count] = hartley_table(count)
    high, low = np_halves(table)
    top = np.concatenate([high, low], axis=1)
    return np.concatenate([top, np.concatenate([high, np.zeros_like(low)], axis=1)], axis=0)


def row_table(table):
    high, low = np_halves(table)
    top = np.concatenate([high, high], axis=1)
    return np.concatenate([top, np.concatenate([low, np.zeros_like(low)], axis=1)], axis=0)


def screened_kernel(count):
    shape = (count // 2, count, 2 * LANES)

    def squared(axis, place):
        index = place(lax.broadcasted_iota(jnp.int32, shape, axis))
        freq = jnp.where(index <= count // 2, index, index - count).astype(F32)
        return freq * freq

    second = 2 * lax.broadcasted_iota(jnp.int32, shape, 0)
    second = second + (lax.broadcasted_iota(jnp.int32, shape, 2) >= LANES).astype(jnp.int32)
    scale = (2.0 * math.pi / CELL) ** 2
    g_two = scale * (squared(0, lambda i: second) + squared(1, lambda i: i) + squared(2, lambda i: i % LANES))
    positive = g_two > 0
    safe = jnp.where(positive, g_two, 1.0)
    value = 4.0 * math.pi / safe * -jnp.expm1(-safe / (4.0 * OMEGA * OMEGA))
    value = jnp.where(positive, value, math.pi / (OMEGA * OMEGA))
    return value / float(count**3)


def to_rows(parts):
    first, second, third = parts
    lane = lax.broadcasted_iota(jnp.int32, first.shape, 1)
    row1 = jnp.where(lane < 32, pltpu.roll(first, 32, 1), pltpu.roll(second, 32, 1))
    row2 = jnp.where(lane < 64, pltpu.roll(second, 64, 1), pltpu.roll(third, 64, 1))
    row3 = pltpu.roll(third, 96, 1)
    return jnp.concatenate([first, row1, row2, row3], axis=0)


def from_rows(plane):
    step = plane.shape[0] // 4
    row0, row1, row2, row3 = (plane[k * step : (k + 1) * step] for k in range(4))
    lane = lax.broadcasted_iota(jnp.int32, row0.shape, 1)
    first = jnp.where(lane < 96, row0, pltpu.roll(row1, 96, 1))
    second = jnp.where(lane < 64, pltpu.roll(row1, 96, 1), pltpu.roll(row2, 64, 1))
    third = jnp.where(lane < 32, pltpu.roll(row2, 64, 1), pltpu.roll(row3, 32, 1))
    return first, second, third


def dot(a, b):
    return jnp.dot(a, b, preferred_element_type=F32)


def along_lanes(value, table):
    out = dot(jnp.concatenate(halves(value), axis=1), table)
    return out[:, :LANES] + out[:, LANES:]


def along_rows(table, value):
    out = dot(table, jnp.concatenate(halves(value), axis=0))
    half = out.shape[0] // 2
    return out[:half] + out[half:]


def pair_kernel(count, sizes, layout, *refs):
    split_in, sums_in, sums_split, terms_in, split_out, twice = layout
    zs, planes = sizes
    slab = 2 * planes
    third, pitch = count // 4, count + GAP
    refs = list(refs)
    place = refs.pop(0)
    partner_hbm = [refs.pop(0) for _ in range(PIECES if split_in else 1)]
    mine_hbm, other_hbm = refs.pop(0), refs.pop(0)
    sums_hbm = refs.pop(0) if sums_in else None
    terms_hbm = refs.pop(0) if terms_in else None
    tables_hbm, coulomb_hbm = refs.pop(0), refs.pop(0)
    sums_out = [refs.pop(0) for _ in range(2 if sums_split else 1)]
    terms_out = [refs.pop(0) for _ in range(PIECES if split_out else 1)]
    partner, orbital, sums, terms, field, tables, coulomb, sem, sem_c = refs
    lanes = tables.at[: 2 * LANES]
    rows_in, rows_mid, rows_out = (
        tables.at[pl.ds(2 * LANES + 2 * count * k, 2 * count), : 2 * count] for k in range(3)
    )
    z, core = place[0], place[1]
    weight = jnp.where((z == 0) | (z == zs - 1), 2.0, 1.0).astype(F32)

    def part(ref, index, size=slab):
        return ref.at[pl.ds(pl.multiple_of(index * size, size), size)]

    def pieces(refs_):
        near = jnp.where(z == 0, 1, z - 1)
        return list(zip(refs_, [z, near, z ^ 2, 6 - z - near - (z ^ 2)]))

    def start(source, target, semaphore, there=None):
        def go():
            pltpu.make_async_copy(source, target, semaphore).start()

        if there is None:
            go()
        else:
            pl.when(there)(go)

    def wait(like_source, like_target, semaphore):
        pltpu.make_async_copy(like_source, like_target, semaphore).wait()

    start(tables_hbm, tables, sem_c.at[1])

    def load(s):
        if split_in:
            for ref, spot in pieces(partner_hbm):
                start(ref, part(partner, s), sem.at[0, s], spot == s)
        else:
            start(part(partner_hbm[0], s), part(partner, s), sem.at[0, s])
        start(mine_hbm.at[s], part(orbital, 2 * s + core, planes), sem.at[1, s])
        start(other_hbm.at[s], part(orbital, 2 * s + 1 - core, planes), sem.at[2, s])

    load(0)
    load(1)

    def density(x):
        parts = []
        for r in range(3):
            rows = pl.ds(r * third, third)
            parts.append(orbital[x, rows, :] * partner[x, rows, :])
        return to_rows(parts)

    group = planes

    def forward(step, carry):
        wait(part(partner, step), part(partner, step), sem.at[0, step])
        wait(part(orbital, 2 * step, planes), part(orbital, 2 * step, planes), sem.at[1, step])
        wait(part(orbital, 2 * step, planes), part(orbital, 2 * step, planes), sem.at[2, step])
        pl.when(step + 2 < zs)(lambda: load(step + 2))
        pl.when(step == zs - 2)(lambda: start(coulomb_hbm, coulomb, sem_c.at[0]))
        base = 2 * group * step
        pairs = [jnp.concatenate([density(base + 2 * g), density(base + 2 * g + 1)], axis=0) for g in range(group)]
        pairs = [along_lanes(both, lanes[...]) for both in pairs]
        pairs = [jnp.concatenate([both[:count], both[count:]], axis=1) for both in pairs]
        pairs = [along_rows(rows_in[...], both) for both in pairs]
        begin = pl.multiple_of(base * pitch, 2 * pitch)
        for g, both in enumerate(pairs):
            field[pl.ds(begin + 2 * g * pitch, count), :] = both[:, :LANES]
            field[pl.ds(begin + (2 * g + 1) * pitch, count), :] = both[:, LANES:]
        return carry

    wait(tables_hbm, tables, sem_c.at[1])
    lax.fori_loop(0, zs, forward, 0)
    for s in range(zs):
        if sums_in:
            start(part(sums_hbm, s), part(sums, s), sem.at[3, s])
        if terms_in:
            start(part(terms_hbm, s), part(terms, s), sem.at[4, s])
    wait(coulomb_hbm, coulomb, sem_c.at[0])

    def middle(step, carry):
        base = 2 * MIDDLE * step
        pairs = [
            jnp.concatenate(
                [field[pl.ds(base + 2 * g + k, count, stride=pitch), :] for k in range(2)], axis=1
            )
            for g in range(MIDDLE)
        ]
        pairs = [along_rows(rows_mid[...], both) for both in pairs]
        pairs = [both * coulomb[MIDDLE * step + g] for g, both in enumerate(pairs)]
        pairs = [along_rows(rows_mid[...], both) for both in pairs]
        for g, both in enumerate(pairs):
            for k in range(2):
                field[pl.ds(base + 2 * g + k, count, stride=pitch), :] = both[:, k * LANES : (k + 1) * LANES]
        return carry

    lax.fori_loop(0, count // 2 // MIDDLE, middle, 0)

    def backward(step, carry):
        if sums_in:
            wait(part(sums_hbm, step), part(sums, step), sem.at[3, step])
        if terms_in:
            wait(part(terms_hbm, step), part(terms, step), sem.at[4, step])
        base = 2 * group * step
        begin = pl.multiple_of(base * pitch, 2 * pitch)
        pairs = [
            jnp.concatenate([field[pl.ds(begin + (2 * g + k) * pitch, count), :] for k in range(2)], axis=1)
            for g in range(group)
        ]
        pairs = [along_rows(rows_out[...], both) for both in pairs]
        pairs = [jnp.concatenate([both[:, :LANES], both[:, LANES:]], axis=0) for both in pairs]
        pairs = [along_lanes(both, lanes[...]) for both in pairs]
        for g, both in enumerate(pairs):
            for k in range(2):
                x = base + 2 * g + k
                for r, value in enumerate(from_rows(both[k * count : (k + 1) * count])):
                    rows = pl.ds(r * third, third)
                    near = partner[x, rows, :] * value
                    sums[x, rows, :] = sums[x, rows, :] + near if sums_in else near
                    far = orbital[x, rows, :] * value
                    far = far * weight if twice else far
                    terms[x, rows, :] = terms[x, rows, :] + far if terms_in else far
        if sums_split:
            start(part(sums, 2 * step + core, planes), sums_out[0].at[step], sem.at[5, step])
            start(part(sums, 2 * step + 1 - core, planes), sums_out[1].at[step], sem.at[6, step])
        else:
            start(part(sums, step), part(sums_out[0], step), sem.at[5, step])
        if split_out:
            for ref, spot in pieces(terms_out):
                start(part(terms, step), ref, sem.at[7, step], spot == step)
        else:
            start(part(terms, step), part(terms_out[0], step), sem.at[7, step])
        return carry

    lax.fori_loop(0, zs, backward, 0)
    for s in range(zs):
        if sums_split:
            for k in range(2):
                wait(part(sums, s, planes), sums_out[k].at[s], sem.at[5 + k, s])
        else:
            wait(part(sums, s), part(sums_out[0], s), sem.at[5, s])
        target = terms_out[0] if split_out else part(terms_out[0], s)
        wait(part(terms, s), target, sem.at[7, s])


def pair_solve(place, partner, mine, other, sums, terms, tables, last_partner, last_orbital, twice=False):
    zs, planes, rows, _ = mine.shape
    count = zs * 2 * planes
    split_in = len(partner) > 1
    layout = (split_in, sums is not None, last_partner, terms is not None, last_orbital and split_in, twice)
    field = jax.ShapeDtypeStruct((count, rows, LANES), F32)
    kinds = [jax.ShapeDtypeStruct(mine.shape, F32)] * 2 if last_partner else [field]
    pieces = [jax.ShapeDtypeStruct(p.shape, F32) for p in partner] if layout[4] else [field]
    more = [a for a in (sums, terms) if a is not None]
    anywhere = pl.BlockSpec(memory_space=pl.ANY)
    block = (count, rows, LANES)
    out = pl.pallas_call(
        functools.partial(pair_kernel, count, (zs, planes), layout),
        in_specs=[pl.BlockSpec(memory_space=pltpu.SMEM)]
        + [anywhere] * (len(partner) + 4 + len(more)),
        out_specs=[anywhere] * (len(kinds) + len(pieces)),
        out_shape=kinds + pieces,
        scratch_shapes=[pltpu.VMEM(block, F32)] * 4
        + [
            pltpu.VMEM((count * (count + GAP), LANES), F32),
            pltpu.VMEM(tables[0].shape, BF16),
            pltpu.VMEM(tables[1].shape, F32),
            pltpu.SemaphoreType.DMA((8, zs)),
            pltpu.SemaphoreType.DMA((2,)),
        ],
        cost_estimate=pl.CostEstimate(
            flops=200 * count**4, bytes_accessed=20 * count * rows * LANES, transcendentals=0
        ),
        compiler_params=pltpu.CompilerParams(vmem_limit_bytes=60 * 1024 * 1024),
    )(place, *partner, mine, other, *more, *tables)
    sums = out[:2] if last_partner else out[0]
    terms = out[len(kinds) :] if layout[4] else out[-1]
    return sums, terms


def make_tables(count):
    table = hartley_table(count)
    order = row_order(count)
    rows = [row_table(t) for t in (table[:, order], table, table[order, :])]
    rows = [np.pad(t, ((0, 0), (0, 2 * LANES - t.shape[1]))) for t in rows]
    return jnp.asarray(np.concatenate([lane_table(count)] + rows, axis=0)), screened_kernel(count)


def piece_row(tile, rows):
    return tile % 3 * (rows // 3) + tile // 3


def pack_kernel(sets, planes, rows, flat, *packed):
    plane = pl.program_id(0)
    for tile in range(rows):
        row = plane * rows + piece_row(tile, rows)
        for runs, out in zip(sets, packed):
            done = 0
            for first, size in runs:
                value = flat[0, first : first + size, tile * LANES : (tile + 1) * LANES]
                out[pl.ds(row + done * planes * rows, size, stride=planes * rows), :] = value
                done += size


def pack(fields, sets):
    planes, number, flat = fields.shape
    rows = flat // LANES
    size = sum(run[1] for run in sets[0])
    out = (size * planes * rows, LANES)
    packed = pl.pallas_call(
        functools.partial(pack_kernel, sets, planes, rows),
        grid=(planes,),
        in_specs=[pl.BlockSpec((1, number, flat), lambda i: (i, 0, 0))],
        out_specs=[pl.BlockSpec(out, lambda i: (0, 0))] * len(sets),
        out_shape=[jax.ShapeDtypeStruct(out, F32)] * len(sets),
        compiler_params=pltpu.CompilerParams(vmem_limit_bytes=32 * 1024 * 1024),
    )(fields)
    return [p.reshape(size, planes, rows, LANES) for p in packed]


def unpack_kernel(order, planes, rows, *refs):
    packed, flat = refs[:-1], refs[-1]
    plane = pl.program_id(0)
    for tile in range(rows):
        row = plane * rows + piece_row(tile, rows)
        runs = [
            packed[k][pl.ds(row + first * planes * rows, size, stride=planes * rows), :] for k, first, size in order
        ]
        value = runs[0] if len(runs) == 1 else jnp.concatenate(runs, axis=0)
        flat[0, :, tile * LANES : (tile + 1) * LANES] = -ALPHA * value


def unpack(fields, order):
    planes, rows = fields[0].shape[1:3]
    number = sum(run[2] for run in order)
    flats = [f.reshape(f.shape[0] * planes * rows, LANES) for f in fields]
    return pl.pallas_call(
        functools.partial(unpack_kernel, order, planes, rows),
        grid=(planes,),
        in_specs=[pl.BlockSpec(f.shape, lambda i: (0, 0), pipeline_mode=pl.Buffered(1)) for f in flats],
        out_specs=pl.BlockSpec((1, number, rows * LANES), lambda i: (i, 0, 0)),
        out_shape=jax.ShapeDtypeStruct((planes, number, rows * LANES), F32),
        compiler_params=pltpu.CompilerParams(vmem_limit_bytes=32 * 1024 * 1024),
    )(*flats)


def swap(value, axis, flip):
    size = lax.axis_size(axis)
    return lax.ppermute(value, axis, [(i, i ^ flip) for i in range(size)])


def along(value, pairs):
    return lax.ppermute(value, "z", pairs)


def tie(values, done):
    return lax.optimization_barrier((values, done))[0]


RIGHT = [(0, 1), (1, 2), (2, 3)]
LEFT = [(1, 0), (2, 1), (3, 2)]


def spread(slab, first):
    z = lax.axis_index("z")
    side, far = [], []

    def both(piece):
        side.append(swap(piece, "band", 1))
        far.append(swap(piece, "band", 2))

    before, after = along(slab, RIGHT), along(slab, LEFT)
    both(slab)
    cross = [swap(side[0], "band", 2)]
    before, after = tie((before, after), (side[-1], far[-1], first, cross))
    near = jnp.where(z == 0, after, before)
    two = along(before, RIGHT[1:]) + along(after, LEFT[:2])
    both(near)
    two = tie(two, (side[-1], far[-1]))
    both(two)
    rest = jnp.where((z == 0) | (z == 3), along(two, [(2, 3), (1, 0)]), after)
    rest = tie(rest, (side[-1], far[-1]))
    both(rest)
    done = (side[3], far[3])
    cross += [swap(tie(far[1], done), "band", 1), swap(tie(side[2], done), "band", 2)]
    cross.append(swap(tie(far[3], cross[1]), "band", 1))
    return [[slab, near, two, rest], side, far, cross]


def local(orbitals):
    n_local, planes, flat = orbitals.shape
    zs, bands, core = lax.axis_size("z"), lax.axis_size("band"), lax.axis_index("core")
    count = planes * zs * 2
    place = jnp.stack([lax.axis_index("z"), core]).astype(jnp.int32)
    tables = make_tables(count)
    square = bands == ROUNDS == 4 and zs == 4 and n_local == 8
    runs = [((2, 4),), ((0, 1), (6, 2), (1, 1))] if square else [((k * zs, zs),) for k in range(n_local // zs)]
    sets = pack(orbitals.swapaxes(0, 1), runs)
    tail = sets[0].shape[2:]
    members, step = (sets[1], zs - 1) if square else (sets[0], 1)
    keep = lax.dynamic_index_in_dim(members, core * step, 0, keepdims=False)
    come = swap(lax.dynamic_index_in_dim(members, (1 - core) * step, 0, keepdims=False), "core", 1)
    slab = jnp.concatenate([jnp.where(core == 0, keep, come), jnp.where(core == 0, come, keep)], axis=0)
    if square:
        return square_local(place, tables, sets, slab)
    every = lax.all_gather(slab, ("band", "z"), axis=0, tiled=True).reshape((bands, count) + tail)
    terms = [None] * ROUNDS
    sums_out = []
    for k, fields in enumerate(sets):
        mine = lax.all_to_all(fields, "z", split_axis=0, concat_axis=0, tiled=True)
        other = swap(mine, "core", 1)
        sums = None
        for turn in range(ROUNDS):
            sums, terms[turn] = pair_solve(
                place, [every[turn]], mine, other, sums, terms[turn], tables, turn == ROUNDS - 1, k == len(sets) - 1
            )
        sums_out.append(sums)
    owner = jnp.concatenate([t[None] for t in terms] + [jnp.zeros((bands - ROUNDS, count) + tail, F32)], axis=0)
    owner = owner.reshape((bands * count,) + tail)
    owner = lax.psum_scatter(owner, ("band", "z"), scatter_dimension=0, tiled=True)
    back = [send_back(core_sum(*sums)) for sums in sums_out]
    back[0] = back[0].at[:PAIR].add(jnp.stack(by_member(owner)))
    return unpack(back, [(k, 0, zs) for k in range(len(back))]).swapaxes(0, 1)


def core_sum(keep, give):
    return keep + swap(give, "core", 1)


def send_back(total):
    return lax.all_to_all(total, "z", split_axis=0, concat_axis=0, tiled=True)


def by_member(owner):
    core, planes = lax.axis_index("core"), owner.shape[0] // 2
    keep = lax.dynamic_slice_in_dim(owner, core * planes, planes)
    come = swap(lax.dynamic_slice_in_dim(owner, (1 - core) * planes, planes), "core", 1)
    return jnp.where(core == 0, keep, come), jnp.where(core == 0, come, keep)


def send_inner(total):
    z = lax.axis_index("z")
    block = lambda index: lax.dynamic_index_in_dim(total, jnp.clip(index, 0, 3), 0, keepdims=False)
    right, left = along(block(z + 1), RIGHT[1:]), along(block(z - 1), LEFT[:2])
    jump = along(block(jnp.where(z == 1, 3, 0)), [(1, 3), (2, 0)])
    own = block(z)
    first = jnp.where(z == 1, own, jnp.where(z == 0, left, jnp.where(z == 2, right, jump)))
    second = jnp.where(z == 2, own, jnp.where(z == 3, right, jnp.where(z == 1, left, jump)))
    return first, second


def square_local(place, tables, sets, slab):
    first = lax.all_to_all(sets[0], "z", split_axis=0, concat_axis=0, tiled=True)
    partners = spread(slab, first)
    mine, other = [first], [swap(first, "core", 1)]

    def pair(k, turn, sums, term=None, after=None, last=False):
        partner = partners[turn] if after is None else tie(partners[turn], after)
        return pair_solve(place, partner, mine[k], other[k], sums, term, tables, last, k == 1, k == 1)

    terms = [None] * ROUNDS
    sums, terms[0] = pair(0, 0, None)
    second = lax.all_to_all(tie(sets[1], partners[0][3]), "z", split_axis=0, concat_axis=0, tiled=True)
    sums, terms[1] = pair(0, 1, sums)
    sums, terms[2] = pair(0, 2, sums, after=partners[3][:3])
    sums, terms[3] = pair(0, 3, sums, last=True)
    mine.append(tie(second, terms[3]))
    other.append(swap(mine[1], "core", 1))
    back = [send_back(core_sum(*sums))]
    z = lax.axis_index("z")
    x_swap = lambda value, done: swap(tie(value, done), "band", 1)
    y_swap = lambda value, done: swap(tie(value, done), "band", 2)
    sums, cross = pair(1, 3, None, terms[3])
    handed3, handed2 = swap(cross[3], "band", 1), swap(cross[2], "band", 2)
    sums, side = pair(1, 1, sums, terms[1])
    done = (handed3, handed2)
    side3, handed0 = x_swap(side[3], done), y_swap(cross[0], done)
    sums, far = pair(1, 2, sums, terms[2], after=done)
    done = (side3, handed0)
    side2, far3 = x_swap(side[2] + handed2, done), y_swap(far[3] + handed3, done)
    sums, own = pair(1, 0, sums, terms[0], after=done + (back[0],), last=True)
    total = core_sum(*sums)
    inner = send_inner(total)
    done = (side2, far3)
    handed1, far2 = x_swap(cross[1], done), y_swap(far[2], done)
    rest = along(own[3] + side3 + far3, [(0, 1), (3, 2)])
    done = (handed1, far2)
    side1, far1 = x_swap(side[1], done), y_swap(far[1] + handed1, done)
    two = tie(own[2] + side2 + far2 + rest, inner)
    after, before = along(two, RIGHT[:2]), along(two, LEFT[1:])
    done = (side1, far1)
    side0, far0 = x_swap(side[0] + handed0, done), y_swap(far[0], done)
    near = own[1] + side1 + far1
    after = jnp.where(z == 0, near, own[3] + side3 + far3 + after)
    after, before = along(after, RIGHT), along(near + before, LEFT)
    owner = by_member(own[0] + side0 + far0 + after + before)
    fields = [back[0], jnp.stack(owner + inner)]
    return unpack(fields, [(1, 0, 2), (0, 0, 4), (1, 2, 2)]).swapaxes(0, 1)


def solution(mesh):
    bands, planes = mesh.devices.shape
    inner = Mesh(mesh.devices.reshape(bands, planes // 2, 2), ("band", "z", "core"))
    placed = P("band", ("z", "core"), None)
    return jax.shard_map(local, mesh=inner, in_specs=(placed,), out_specs=placed, check_vma=False)
```

```python
import functools
import math

import jax
import jax.numpy as jnp
import numpy as np
from jax import lax
from jax.experimental import pallas as pl
from jax.experimental.pallas import tpu as pltpu
from jax.sharding import Mesh, PartitionSpec as P

PAIR = 2
ROUNDS = 4
OMEGA = 0.106
CELL = 41.05
ALPHA = 0.25
LANES = 128
F32 = jnp.float32
BF16 = jnp.bfloat16
MIDDLE = 12
GAP = 8
PIECES = 4


def hartley_table(count):
    index = np.arange(count)
    angle = (index[:, None] * index[None, :] % count).astype(np.float64) * (2.0 * math.pi / count)
    return (np.cos(angle) + np.sin(angle)).astype(np.float32)


def halves(value):
    high = value.astype(BF16)
    return high, (value - high.astype(F32)).astype(BF16)


def np_halves(value):
    high = value.astype(BF16)
    return high, (value - high.astype(np.float32)).astype(BF16)


def row_order(count):
    return np.arange(count).reshape(count // 4, 4).T.reshape(-1)


def lane_table(count):
    table = np.zeros((LANES, LANES), np.float32)
    table[:count, :count] = hartley_table(count)
    high, low = np_halves(table)
    top = np.concatenate([high, low], axis=1)
    return np.concatenate([top, np.concatenate([high, np.zeros_like(low)], axis=1)], axis=0)


def row_table(table):
    high, low = np_halves(table)
    top = np.concatenate([high, high], axis=1)
    return np.concatenate([top, np.concatenate([low, np.zeros_like(low)], axis=1)], axis=0)


def screened_kernel(count):
    shape = (count // 2, count, 2 * LANES)

    def squared(axis, place):
        index = place(lax.broadcasted_iota(jnp.int32, shape, axis))
        freq = jnp.where(index <= count // 2, index, index - count).astype(F32)
        return freq * freq

    second = 2 * lax.broadcasted_iota(jnp.int32, shape, 0)
    second = second + (lax.broadcasted_iota(jnp.int32, shape, 2) >= LANES).astype(jnp.int32)
    scale = (2.0 * math.pi / CELL) ** 2
    g_two = scale * (squared(0, lambda i: second) + squared(1, lambda i: i) + squared(2, lambda i: i % LANES))
    positive = g_two > 0
    safe = jnp.where(positive, g_two, 1.0)
    value = 4.0 * math.pi / safe * -jnp.expm1(-safe / (4.0 * OMEGA * OMEGA))
    value = jnp.where(positive, value, math.pi / (OMEGA * OMEGA))
    return value / float(count**3)


def to_rows(parts):
    first, second, third = parts
    lane = lax.broadcasted_iota(jnp.int32, first.shape, 1)
    row1 = jnp.where(lane < 32, pltpu.roll(first, 32, 1), pltpu.roll(second, 32, 1))
    row2 = jnp.where(lane < 64, pltpu.roll(second, 64, 1), pltpu.roll(third, 64, 1))
    row3 = pltpu.roll(third, 96, 1)
    return jnp.concatenate([first, row1, row2, row3], axis=0)


def from_rows(plane):
    step = plane.shape[0] // 4
    row0, row1, row2, row3 = (plane[k * step : (k + 1) * step] for k in range(4))
    lane = lax.broadcasted_iota(jnp.int32, row0.shape, 1)
    first = jnp.where(lane < 96, row0, pltpu.roll(row1, 96, 1))
    second = jnp.where(lane < 64, pltpu.roll(row1, 96, 1), pltpu.roll(row2, 64, 1))
    third = jnp.where(lane < 32, pltpu.roll(row2, 64, 1), pltpu.roll(row3, 32, 1))
    return first, second, third


def dot(a, b):
    return jnp.dot(a, b, preferred_element_type=F32)


def along_lanes(value, table):
    out = dot(jnp.concatenate(halves(value), axis=1), table)
    return out[:, :LANES] + out[:, LANES:]


def along_rows(table, value):
    out = dot(table, jnp.concatenate(halves(value), axis=0))
    half = out.shape[0] // 2
    return out[:half] + out[half:]


def pair_kernel(count, sizes, layout, *refs):
    split_in, sums_in, sums_split, terms_in, split_out, twice = layout
    zs, planes = sizes
    slab = 2 * planes
    third, pitch = count // 4, count + GAP
    refs = list(refs)
    place = refs.pop(0)
    partner_hbm = [refs.pop(0) for _ in range(PIECES if split_in else 1)]
    mine_hbm, other_hbm = refs.pop(0), refs.pop(0)
    sums_hbm = refs.pop(0) if sums_in else None
    terms_hbm = refs.pop(0) if terms_in else None
    tables_hbm, coulomb_hbm = refs.pop(0), refs.pop(0)
    sums_out = [refs.pop(0) for _ in range(2 if sums_split else 1)]
    terms_out = [refs.pop(0) for _ in range(PIECES if split_out else 1)]
    partner, orbital, sums, terms, field, tables, coulomb, sem, sem_c = refs
    lanes = tables.at[: 2 * LANES]
    rows_in, rows_mid, rows_out = (
        tables.at[pl.ds(2 * LANES + 2 * count * k, 2 * count), : 2 * count] for k in range(3)
    )
    z, core = place[0], place[1]
    weight = jnp.where((z == 0) | (z == zs - 1), 2.0, 1.0).astype(F32)

    def part(ref, index, size=slab):
        return ref.at[pl.ds(pl.multiple_of(index * size, size), size)]

    def pieces(refs_):
        near = jnp.where(z == 0, 1, z - 1)
        return list(zip(refs_, [z, near, z ^ 2, 6 - z - near - (z ^ 2)]))

    def start(source, target, semaphore, there=None):
        def go():
            pltpu.make_async_copy(source, target, semaphore).start()

        if there is None:
            go()
        else:
            pl.when(there)(go)

    def wait(like_source, like_target, semaphore):
        pltpu.make_async_copy(like_source, like_target, semaphore).wait()

    start(tables_hbm, tables, sem_c.at[1])

    def load(s):
        if split_in:
            for ref, spot in pieces(partner_hbm):
                start(ref, part(partner, s), sem.at[0, s], spot == s)
        else:
            start(part(partner_hbm[0], s), part(partner, s), sem.at[0, s])
        start(mine_hbm.at[s], part(orbital, 2 * s + core, planes), sem.at[1, s])
        start(other_hbm.at[s], part(orbital, 2 * s + 1 - core, planes), sem.at[2, s])

    load(0)
    load(1)

    def density(x):
        parts = []
        for r in range(3):
            rows = pl.ds(r * third, third)
            parts.append(orbital[x, rows, :] * partner[x, rows, :])
        return to_rows(parts)

    group = planes

    def forward(step, carry):
        wait(part(partner, step), part(partner, step), sem.at[0, step])
        wait(part(orbital, 2 * step, planes), part(orbital, 2 * step, planes), sem.at[1, step])
        wait(part(orbital, 2 * step, planes), part(orbital, 2 * step, planes), sem.at[2, step])
        pl.when(step + 2 < zs)(lambda: load(step + 2))
        pl.when(step == zs - 2)(lambda: start(coulomb_hbm, coulomb, sem_c.at[0]))
        base = 2 * group * step
        pairs = [jnp.concatenate([density(base + 2 * g), density(base + 2 * g + 1)], axis=0) for g in range(group)]
        pairs = [along_lanes(both, lanes[...]) for both in pairs]
        pairs = [jnp.concatenate([both[:count], both[count:]], axis=1) for both in pairs]
        pairs = [along_rows(rows_in[...], both) for both in pairs]
        begin = pl.multiple_of(base * pitch, 2 * pitch)
        for g, both in enumerate(pairs):
            field[pl.ds(begin + 2 * g * pitch, count), :] = both[:, :LANES]
            field[pl.ds(begin + (2 * g + 1) * pitch, count), :] = both[:, LANES:]
        return carry

    wait(tables_hbm, tables, sem_c.at[1])
    lax.fori_loop(0, zs, forward, 0)
    for s in range(zs):
        if sums_in:
            start(part(sums_hbm, s), part(sums, s), sem.at[3, s])
        if terms_in:
            start(part(terms_hbm, s), part(terms, s), sem.at[4, s])
    wait(coulomb_hbm, coulomb, sem_c.at[0])

    def middle(step, carry):
        base = 2 * MIDDLE * step
        pairs = [
            jnp.concatenate(
                [field[pl.ds(base + 2 * g + k, count, stride=pitch), :] for k in range(2)], axis=1
            )
            for g in range(MIDDLE)
        ]
        pairs = [along_rows(rows_mid[...], both) for both in pairs]
        pairs = [both * coulomb[MIDDLE * step + g] for g, both in enumerate(pairs)]
        pairs = [along_rows(rows_mid[...], both) for both in pairs]
        for g, both in enumerate(pairs):
            for k in range(2):
                field[pl.ds(base + 2 * g + k, count, stride=pitch), :] = both[:, k * LANES : (k + 1) * LANES]
        return carry

    lax.fori_loop(0, count // 2 // MIDDLE, middle, 0)

    def backward(step, carry):
        if sums_in:
            wait(part(sums_hbm, step), part(sums, step), sem.at[3, step])
        if terms_in:
            wait(part(terms_hbm, step), part(terms, step), sem.at[4, step])
        base = 2 * group * step
        begin = pl.multiple_of(base * pitch, 2 * pitch)
        pairs = [
            jnp.concatenate([field[pl.ds(begin + (2 * g + k) * pitch, count), :] for k in range(2)], axis=1)
            for g in range(group)
        ]
        pairs = [along_rows(rows_out[...], both) for both in pairs]
        pairs = [jnp.concatenate([both[:, :LANES], both[:, LANES:]], axis=0) for both in pairs]
        pairs = [along_lanes(both, lanes[...]) for both in pairs]
        for g, both in enumerate(pairs):
            for k in range(2):
                x = base + 2 * g + k
                for r, value in enumerate(from_rows(both[k * count : (k + 1) * count])):
                    rows = pl.ds(r * third, third)
                    near = partner[x, rows, :] * value
                    sums[x, rows, :] = sums[x, rows, :] + near if sums_in else near
                    far = orbital[x, rows, :] * value
                    far = far * weight if twice else far
                    terms[x, rows, :] = terms[x, rows, :] + far if terms_in else far
        if sums_split:
            start(part(sums, 2 * step + core, planes), sums_out[0].at[step], sem.at[5, step])
            start(part(sums, 2 * step + 1 - core, planes), sums_out[1].at[step], sem.at[6, step])
        else:
            start(part(sums, step), part(sums_out[0], step), sem.at[5, step])
        if split_out:
            for ref, spot in pieces(terms_out):
                start(part(terms, step), ref, sem.at[7, step], spot == step)
        else:
            start(part(terms, step), part(terms_out[0], step), sem.at[7, step])
        return carry

    lax.fori_loop(0, zs, backward, 0)
    for s in range(zs):
        if sums_split:
            for k in range(2):
                wait(part(sums, s, planes), sums_out[k].at[s], sem.at[5 + k, s])
        else:
            wait(part(sums, s), part(sums_out[0], s), sem.at[5, s])
        target = terms_out[0] if split_out else part(terms_out[0], s)
        wait(part(terms, s), target, sem.at[7, s])


def pair_solve(place, partner, mine, other, sums, terms, tables, last_partner, last_orbital, twice=False):
    zs, planes, rows, _ = mine.shape
    count = zs * 2 * planes
    split_in = len(partner) > 1
    layout = (split_in, sums is not None, last_partner, terms is not None, last_orbital and split_in, twice)
    field = jax.ShapeDtypeStruct((count, rows, LANES), F32)
    kinds = [jax.ShapeDtypeStruct(mine.shape, F32)] * 2 if last_partner else [field]
    pieces = [jax.ShapeDtypeStruct(p.shape, F32) for p in partner] if layout[4] else [field]
    more = [a for a in (sums, terms) if a is not None]
    anywhere = pl.BlockSpec(memory_space=pl.ANY)
    block = (count, rows, LANES)
    out = pl.pallas_call(
        functools.partial(pair_kernel, count, (zs, planes), layout),
        in_specs=[pl.BlockSpec(memory_space=pltpu.SMEM)]
        + [anywhere] * (len(partner) + 4 + len(more)),
        out_specs=[anywhere] * (len(kinds) + len(pieces)),
        out_shape=kinds + pieces,
        scratch_shapes=[pltpu.VMEM(block, F32)] * 4
        + [
            pltpu.VMEM(((count + 1) * (count + GAP), LANES), F32),
            pltpu.VMEM(tables[0].shape, BF16),
            pltpu.VMEM(tables[1].shape, F32),
            pltpu.SemaphoreType.DMA((8, zs)),
            pltpu.SemaphoreType.DMA((2,)),
        ],
        cost_estimate=pl.CostEstimate(
            flops=200 * count**4, bytes_accessed=20 * count * rows * LANES, transcendentals=0
        ),
        compiler_params=pltpu.CompilerParams(vmem_limit_bytes=60 * 1024 * 1024),
    )(place, *partner, mine, other, *more, *tables)
    sums = out[:2] if last_partner else out[0]
    terms = out[len(kinds) :] if layout[4] else out[-1]
    return sums, terms


def make_tables(count):
    table = hartley_table(count)
    order = row_order(count)
    rows = [row_table(t) for t in (table[:, order], table, table[order, :])]
    rows = [np.pad(t, ((0, 0), (0, 2 * LANES - t.shape[1]))) for t in rows]
    return jnp.asarray(np.concatenate([lane_table(count)] + rows, axis=0)), screened_kernel(count)


def piece_row(tile, rows):
    return tile % 3 * (rows // 3) + tile // 3


def pack_kernel(planes, rows, flat, packed):
    plane = pl.program_id(0)
    for tile in range(rows):
        row = plane * rows + piece_row(tile, rows)
        value = flat[0, :, tile * LANES : (tile + 1) * LANES]
        packed[pl.ds(row, flat.shape[1], stride=planes * rows), :] = value


def pack(fields):
    planes, number, flat = fields.shape
    rows = flat // LANES
    out = (number * planes * rows, LANES)
    packed = pl.pallas_call(
        functools.partial(pack_kernel, planes, rows),
        grid=(planes,),
        in_specs=[pl.BlockSpec((1, number, flat), lambda i: (i, 0, 0))],
        out_specs=pl.BlockSpec(out, lambda i: (0, 0)),
        out_shape=jax.ShapeDtypeStruct(out, F32),
        compiler_params=pltpu.CompilerParams(vmem_limit_bytes=32 * 1024 * 1024),
    )(fields)
    return packed.reshape(number, planes, rows, LANES)


def unpack_kernel(planes, rows, packed, flat):
    plane = pl.program_id(0)
    for tile in range(rows):
        row = plane * rows + piece_row(tile, rows)
        value = packed[pl.ds(row, flat.shape[1], stride=planes * rows), :]
        flat[0, :, tile * LANES : (tile + 1) * LANES] = -ALPHA * value


def unpack(fields):
    number, planes, rows, _ = fields.shape
    whole = (number * planes * rows, LANES)
    return pl.pallas_call(
        functools.partial(unpack_kernel, planes, rows),
        grid=(planes,),
        in_specs=[pl.BlockSpec(whole, lambda i: (0, 0), pipeline_mode=pl.Buffered(1))],
        out_specs=pl.BlockSpec((1, number, rows * LANES), lambda i: (i, 0, 0)),
        out_shape=jax.ShapeDtypeStruct((planes, number, rows * LANES), F32),
        compiler_params=pltpu.CompilerParams(vmem_limit_bytes=32 * 1024 * 1024),
    )(fields.reshape(whole))


def swap(value, axis, flip):
    size = lax.axis_size(axis)
    return lax.ppermute(value, axis, [(i, i ^ flip) for i in range(size)])


def along(value, pairs):
    return lax.ppermute(value, "z", pairs)


def tie(values, done):
    return lax.optimization_barrier((values, done))[0]


RIGHT = [(0, 1), (1, 2), (2, 3)]
LEFT = [(1, 0), (2, 1), (3, 2)]


def spread(slab, first):
    z = lax.axis_index("z")
    side, far = [], []

    def both(piece):
        side.append(swap(piece, "band", 1))
        far.append(swap(piece, "band", 2))

    before, after = along(slab, RIGHT), along(slab, LEFT)
    both(slab)
    cross = [swap(side[0], "band", 2)]
    before, after = tie((before, after), (side[-1], far[-1], first, cross))
    near = jnp.where(z == 0, after, before)
    two = along(before, RIGHT[1:]) + along(after, LEFT[:2])
    both(near)
    two = tie(two, (side[-1], far[-1]))
    both(two)
    rest = jnp.where((z == 0) | (z == 3), along(two, [(2, 3), (1, 0)]), after)
    rest = tie(rest, (side[-1], far[-1]))
    both(rest)
    done = (side[3], far[3])
    cross += [swap(tie(far[1], done), "band", 1), swap(tie(side[2], done), "band", 2)]
    cross.append(swap(tie(far[3], cross[1]), "band", 1))
    return [[slab, near, two, rest], side, far, cross]


def local(orbitals):
    n_local, planes, flat = orbitals.shape
    zs, bands, core = lax.axis_size("z"), lax.axis_size("band"), lax.axis_index("core")
    count = planes * zs * 2
    place = jnp.stack([lax.axis_index("z"), core]).astype(jnp.int32)
    tables = make_tables(count)
    square = bands == ROUNDS == 4 and zs == 4 and n_local == 8
    packed = pack(orbitals.swapaxes(0, 1))
    if square:
        sets = [packed[2:6], jnp.concatenate([packed[0:1], packed[6:8], packed[1:2]], axis=0)]
    else:
        sets = [packed[k : k + zs] for k in range(0, n_local, zs)]
    tail = sets[0].shape[2:]
    keep = lax.dynamic_index_in_dim(packed, core, 0, keepdims=False)
    come = swap(lax.dynamic_index_in_dim(packed, 1 - core, 0, keepdims=False), "core", 1)
    slab = jnp.concatenate([jnp.where(core == 0, keep, come), jnp.where(core == 0, come, keep)], axis=0)
    if square:
        return square_local(place, tables, sets, slab)
    every = lax.all_gather(slab, ("band", "z"), axis=0, tiled=True).reshape((bands, count) + tail)
    terms = [None] * ROUNDS
    sums_out = []
    for k, fields in enumerate(sets):
        mine = lax.all_to_all(fields, "z", split_axis=0, concat_axis=0, tiled=True)
        other = swap(mine, "core", 1)
        sums = None
        for turn in range(ROUNDS):
            sums, terms[turn] = pair_solve(
                place, [every[turn]], mine, other, sums, terms[turn], tables, turn == ROUNDS - 1, k == len(sets) - 1
            )
        sums_out.append(sums)
    owner = jnp.concatenate([t[None] for t in terms] + [jnp.zeros((bands - ROUNDS, count) + tail, F32)], axis=0)
    owner = owner.reshape((bands * count,) + tail)
    owner = lax.psum_scatter(owner, ("band", "z"), scatter_dimension=0, tiled=True)
    back = [send_back(core_sum(*sums)) for sums in sums_out]
    back[0] = back[0].at[:PAIR].add(jnp.stack(by_member(owner)))
    return unpack(jnp.concatenate(back, axis=0)).swapaxes(0, 1)


def core_sum(keep, give):
    return keep + swap(give, "core", 1)


def send_back(total):
    return lax.all_to_all(total, "z", split_axis=0, concat_axis=0, tiled=True)


def by_member(owner):
    core, planes = lax.axis_index("core"), owner.shape[0] // 2
    keep = lax.dynamic_slice_in_dim(owner, core * planes, planes)
    come = swap(lax.dynamic_slice_in_dim(owner, (1 - core) * planes, planes), "core", 1)
    return jnp.where(core == 0, keep, come), jnp.where(core == 0, come, keep)


def send_inner(total):
    z = lax.axis_index("z")
    block = lambda index: lax.dynamic_index_in_dim(total, jnp.clip(index, 0, 3), 0, keepdims=False)
    right, left = along(block(z + 1), RIGHT[1:]), along(block(z - 1), LEFT[:2])
    jump = along(block(jnp.where(z == 1, 3, 0)), [(1, 3), (2, 0)])
    own = block(z)
    first = jnp.where(z == 1, own, jnp.where(z == 0, left, jnp.where(z == 2, right, jump)))
    second = jnp.where(z == 2, own, jnp.where(z == 3, right, jnp.where(z == 1, left, jump)))
    return first, second


def square_local(place, tables, sets, slab):
    first = lax.all_to_all(sets[0], "z", split_axis=0, concat_axis=0, tiled=True)
    partners = spread(slab, first)
    mine, other = [first], [swap(first, "core", 1)]

    def pair(k, turn, sums, term=None, after=None, last=False):
        partner = partners[turn] if after is None else tie(partners[turn], after)
        return pair_solve(place, partner, mine[k], other[k], sums, term, tables, last, k == 1, k == 1)

    terms = [None] * ROUNDS
    sums, terms[0] = pair(0, 0, None)
    second = lax.all_to_all(tie(sets[1], partners[0][3]), "z", split_axis=0, concat_axis=0, tiled=True)
    sums, terms[1] = pair(0, 1, sums)
    sums, terms[2] = pair(0, 2, sums, after=partners[3][:3])
    sums, terms[3] = pair(0, 3, sums, last=True)
    mine.append(tie(second, terms[3]))
    other.append(swap(mine[1], "core", 1))
    back = [send_back(core_sum(*sums))]
    z = lax.axis_index("z")
    x_swap = lambda value, done: swap(tie(value, done), "band", 1)
    y_swap = lambda value, done: swap(tie(value, done), "band", 2)
    sums, cross = pair(1, 3, None, terms[3])
    handed3, handed2 = swap(cross[3], "band", 1), swap(cross[2], "band", 2)
    sums, side = pair(1, 1, sums, terms[1])
    done = (handed3, handed2)
    side3, handed0 = x_swap(side[3], done), y_swap(cross[0], done)
    sums, far = pair(1, 2, sums, terms[2], after=done)
    done = (side3, handed0)
    side2, far3 = x_swap(side[2] + handed2, done), y_swap(far[3] + handed3, done)
    sums, own = pair(1, 0, sums, terms[0], after=done + (back[0],), last=True)
    total = core_sum(*sums)
    inner = send_inner(total)
    done = (side2, far3)
    handed1, far2 = x_swap(cross[1], done), y_swap(far[2], done)
    rest = along(own[3] + side3 + far3, [(0, 1), (3, 2)])
    done = (handed1, far2)
    side1, far1 = x_swap(side[1], done), y_swap(far[1] + handed1, done)
    two = tie(own[2] + side2 + far2 + rest, inner)
    after, before = along(two, RIGHT[:2]), along(two, LEFT[1:])
    done = (side1, far1)
    side0, far0 = x_swap(side[0] + handed0, done), y_swap(far[0], done)
    near = own[1] + side1 + far1
    after = jnp.where(z == 0, near, own[3] + side3 + far3 + after)
    after, before = along(after, RIGHT), along(near + before, LEFT)
    owner = by_member(own[0] + side0 + far0 + after + before)
    return unpack(jnp.concatenate([jnp.stack(owner), back[0], jnp.stack(inner)], axis=0)).swapaxes(0, 1)


def solution(mesh):
    bands, planes = mesh.devices.shape
    inner = Mesh(mesh.devices.reshape(bands, planes // 2, 2), ("band", "z", "core"))
    placed = P("band", ("z", "core"), None)
    return jax.shard_map(local, mesh=inner, in_specs=(placed,), out_specs=placed, check_vma=False)
```
